512 devices in a mesh: dp: 8 (over y_lo, core), expert: 64 (over y_hi, x, z).
Axes of the slice: x: 4, y: 8 (y_hi: 2, y_lo: 4; y = y_hi * 4 + y_lo), z: 8, core: 2. Of those that a mesh axis runs over, the one named last changes fastest.
Arguments:
- tokens: bfloat16 [512, 192, 1280], P(('dp', 'expert')), may hold values from -64 to 64
- grad_out: bfloat16 [512, 192, 1280], P(('dp', 'expert')), may hold values from -6 to 6
- router: bfloat16 [1280, 64], replicated, may hold values from -0.1118034 to 0.1118034
- w_in: bfloat16 [64, 2560, 1280], P('expert', 'dp'), may hold values from -0.15625 to 0.15625
- w_out: bfloat16 [64, 2560, 1280], P('expert', 'dp'), may hold values from -0.125 to 0.125
Outputs:
- d_tokens: bfloat16 [512, 192, 1280], P(('dp', 'expert'))
- d_router: bfloat16 [1280, 64], replicated
- d_w_in: bfloat16 [64, 2560, 1280], P('expert', 'dp')
- d_w_out: bfloat16 [64, 2560, 1280], P('expert', 'dp')
The draws below stay inside these ranges and needn't reach their ends.
All inputs are finite; a program needn't handle non-finite values.
Results may differ from the reference program's by a relative error of at most 0.019.
Values may be sent and summed in bfloat16 or wider, within the bound.
No kernel may reach another device: no remote copies, remote signals or barrier semaphores. Data moves between devices by JAX's collectives and lax.ppermute only.
A program may use at most 64 MiB of HBM per device.

```python
import math
import jax
import jax.numpy as jnp
from jax import lax

D = 1280
HID = 2560
PATCHES = 192
EXPERTS = 64
IMAGES = 512
HID_DEV = 320
N_DP = 8


def router_parts(key):
    subkeys = jax.random.split(key, 3)
    column_gains = jnp.exp(jax.random.uniform(subkeys[0], (EXPERTS,), jnp.float32, math.log(0.5), math.log(2.0)))
    amplitude = (0.5 * D ** (-0.5) * column_gains).astype(jnp.bfloat16).astype(jnp.float32)
    normals = jnp.clip(jax.random.normal(subkeys[2], (D, EXPERTS), jnp.float32), -4.0, 4.0)
    row_index = jnp.arange(D, dtype=jnp.int32)[:, None]
    col_index = jnp.arange(EXPERTS, dtype=jnp.int32)[None, :]
    shared_bits = jnp.bitwise_and(row_index, col_index)
    parity = jnp.zeros((D, EXPERTS), jnp.int32)
    for bit_index in range(16):
        parity = parity + jnp.bitwise_and(jnp.right_shift(shared_bits, bit_index), 1)
    return (amplitude, normals)


def draw_router(key, part):
    amplitude, normals = router_parts(key)
    table = normals * amplitude[None, :]
    return table.astype(jnp.bfloat16)


def draw_tokens(key, part):
    key = jax.random.fold_in(key, 12)
    subkeys = jax.random.split(key, 2)
    position = jnp.arange(PATCHES, dtype=jnp.int32)
    row_scale = jnp.exp(jax.random.uniform(subkeys[0], (IMAGES, PATCHES), jnp.float32, math.log(0.4), math.log(1.2)))
    row_scale = row_scale * (1.0 + 2.0 * position.astype(jnp.float32) / PATCHES)[None, :]
    noise = jnp.clip(jax.random.normal(subkeys[1], (IMAGES, PATCHES, D), jnp.float32), -4.0, 4.0)
    values = noise * row_scale[:, :, None]
    return values.astype(jnp.bfloat16)


def steps_of(key, extent, shards, smallest, largest):
    factor_of = 1.0
    for dim, blocks in shards:
        heights = jax.random.uniform(jax.random.fold_in(jax.random.fold_in(key, 6), dim), (blocks,), jnp.float32, smallest / len(shards), largest / len(shards))
        factor_of = factor_of * jnp.repeat(jnp.exp(heights), extent[dim] // blocks).reshape((-1,) + (1,) * (len(extent) - 1 - dim))
    return factor_of


def scatter_about(rng, extent, scale, bound, shards=(), kind=jnp.bfloat16):
    loudness = steps_of(rng, extent, shards, -0.22, 0.18) if shards else 1.0
    entries = jax.random.normal(rng, extent, jnp.float32) * scale * loudness
    return jnp.minimum(jnp.maximum(entries, -bound), bound).astype(kind)


def setup_inputs(seed: int = 0) -> dict:
    key_list = jax.random.split(jax.random.key(seed), 6)
    return {
        "tokens": draw_tokens(jax.random.fold_in(key_list[5], 71), 0),
        "grad_out": scatter_about(key_list[1], (IMAGES, PATCHES, D), 1.0, 6.0, ((0, 512),)),
        "router": draw_router(jax.random.fold_in(key_list[5], 71), 0),
        "w_in": scatter_about(key_list[3], (EXPERTS, HID, D), D ** -0.5, 0.15625, ((0, 64), (1, 8))),
        "w_out": scatter_about(key_list[4], (EXPERTS, HID, D), HID ** -0.5, 0.125, ((0, 64), (1, 8))),
    }


def gelu_back(preact, upstream):
    return jax.vjp(jax.nn.gelu, preact)[1](upstream)[0]

def rounded(value):
    return lax.optimization_barrier(value.astype(jnp.bfloat16)).astype(jnp.float32)

def reference(tokens, grad_out, router, w_in, w_out):
    token_float = tokens.astype(jnp.float32)
    grad_float = grad_out.astype(jnp.float32)
    router_float = router.astype(jnp.float32)
    logits = jnp.einsum('imd,ds->ims', token_float, router_float)
    dispatch = jax.nn.softmax(logits, axis=1)
    combine = jax.nn.softmax(logits, axis=2)
    dispatch_cast = dispatch.astype(jnp.bfloat16).astype(jnp.float32)
    combine_cast = combine.astype(jnp.bfloat16).astype(jnp.float32)
    slot_in = jnp.einsum('ims,imd->isd', dispatch_cast, token_float).astype(jnp.bfloat16).astype(jnp.float32)
    slot_grad = jnp.einsum('ims,imd->isd', combine_cast, grad_float).astype(jnp.bfloat16).astype(jnp.float32)
    w_in_float = w_in.astype(jnp.float32)
    w_out_float = w_out.astype(jnp.float32)
    preact = jnp.einsum('isd,shd->ish', slot_in, w_in_float)
    hidden = jax.nn.gelu(preact).astype(jnp.bfloat16).astype(jnp.float32)
    hidden_grad = jnp.einsum('isd,shd->ish', slot_grad, w_out_float)
    preact_grad = gelu_back(preact, hidden_grad).astype(jnp.bfloat16).astype(jnp.float32)
    d_w_out = jnp.einsum('ish,isd->shd', hidden, slot_grad).astype(jnp.bfloat16)
    d_w_in = jnp.einsum('ish,isd->shd', preact_grad, slot_in).astype(jnp.bfloat16)
    summed_out = jnp.zeros((IMAGES, EXPERTS, D), jnp.float32)
    summed_back = jnp.zeros((IMAGES, EXPERTS, D), jnp.float32)
    for shard_index in range(N_DP):
        start_row = shard_index * HID_DEV
        stop_row = start_row + HID_DEV
        summed_out = summed_out + rounded(jnp.einsum('ish,shd->isd', hidden[:, :, start_row:stop_row], w_out_float[:, start_row:stop_row]))
        summed_back = summed_back + rounded(jnp.einsum('ish,shd->isd', preact_grad[:, :, start_row:stop_row], w_in_float[:, start_row:stop_row]))
    slot_out = summed_out.astype(jnp.bfloat16).astype(jnp.float32)
    slot_in_grad = summed_back.astype(jnp.bfloat16).astype(jnp.float32)
    combine_grad = jnp.einsum('imd,isd->ims', grad_float, slot_out)
    combine_logit = combine * (combine_grad - lax.optimization_barrier(jnp.sum(combine * combine_grad, axis=2, keepdims=True)))
    dispatch_grad = jnp.einsum('imd,isd->ims', token_float, slot_in_grad)
    slot_stat = jnp.einsum('isd,isd->is', slot_in, slot_in_grad)
    logit_grad = (dispatch * (dispatch_grad - slot_stat[:, None, :]) + combine_logit).astype(jnp.bfloat16).astype(jnp.float32)
    d_tokens = (jnp.einsum('ims,ds->imd', logit_grad, router_float) + jnp.einsum('ims,isd->imd', dispatch_cast, slot_in_grad)).astype(jnp.bfloat16)
    d_router = jnp.einsum('imd,ims->ds', token_float, logit_grad).astype(jnp.bfloat16)
    return (d_tokens, d_router, d_w_in, d_w_out)
```

```python
import jax
import jax.numpy as jnp
from jax import lax
from jax.sharding import Mesh, PartitionSpec as P

SWAP = [(0, 1), (1, 0)]
DP = ("y_lo", "core")
EXPERT = ("y_hi", "x", "z")
PLANE = ("x", "z")
COLUMN = ("y_lo", "y_hi")
RING = ("y_lo", "x")
REST = ("core", "y_hi", "z")
BF = jnp.bfloat16
F32 = jnp.float32


def gelu_back(preact, upstream):
    return jax.vjp(jax.nn.gelu, preact)[1](upstream)[0]


def exchange(blocks, axes):
    return lax.all_to_all(blocks, axes, split_axis=0, concat_axis=0, tiled=True)


def swap(value):
    return lax.ppermute(value, "core", SWAP)


def dot(spec, left, right):
    return jnp.einsum(spec, left, right, preferred_element_type=F32)


def local(tokens, grad_out, router, w_in, w_out):
    tokens, grad_out, w_in, w_out = tokens[0], grad_out[0], w_in[0], w_out[0]
    first = lax.axis_index("core") == 0
    weight_kept = jnp.where(first, w_in, w_out)
    weight_got = swap(jnp.where(first, w_out, w_in))
    weight = jnp.concatenate(
        [jnp.where(first, weight_kept, weight_got), jnp.where(first, weight_got, weight_kept)]
    )
    router = router.reshape(1280, 2, 32).swapaxes(1, 2).reshape(1280, 64)
    logits = dot("md,ds->ms", tokens, router)
    dispatch = jax.nn.softmax(logits, axis=0)
    combine = jax.nn.softmax(logits, axis=1)
    dispatch_cast = dispatch.astype(BF)
    own_in = dot("ms,md->sd", dispatch_cast, tokens).astype(BF)
    own_grad = dot("ms,md->sd", combine.astype(BF), grad_out).astype(BF)
    got = swap(jnp.where(first, own_grad, own_in))
    pair = jnp.stack(
        [jnp.where(first, own_in, got), jnp.where(first, got, own_grad)], axis=1
    )
    blocks = pair.reshape(32, 4, 1280)
    moved = exchange(blocks, PLANE).reshape(32, 2, 2, 1280)
    moved = moved.swapaxes(0, 1).reshape(1, 2, 64, 1280)
    rows = exchange(
        jnp.broadcast_to(moved, (4, 2, 64, 1280)).reshape(8, 64, 1280), COLUMN
    ).reshape(512, 1280)
    act = dot("id,hd->ih", rows, weight)
    other = swap(jnp.where(first, jax.nn.gelu(act), act).astype(BF))
    hid = jnp.where(first, gelu_back(act, other.astype(F32)).astype(BF), other)
    partial = dot("ih,hd->id", hid, weight).astype(BF)
    d_weight = dot("ih,id->hd", hid, rows).astype(BF)
    parts = exchange(partial.reshape(8, 64, 1280), COLUMN).reshape(4, 2, 32, 2, 1280)
    summed = jnp.sum(parts.astype(F32), axis=0).astype(BF)
    back = exchange(
        summed.swapaxes(0, 1).reshape(32, 4, 1280), PLANE
    ).reshape(64, 2, 1280)
    kept = jnp.where(first, back[:, 0], back[:, 1])
    got = swap(jnp.where(first, back[:, 1], back[:, 0]))
    slot_in_grad = jnp.where(first, kept, got)
    slot_out = jnp.where(first, got, kept)
    slot_stat = jnp.sum(own_in.astype(F32) * slot_in_grad.astype(F32), axis=1)
    combine_grad = dot("md,sd->ms", grad_out, slot_out)
    combine_logit = combine * (
        combine_grad - jnp.sum(combine * combine_grad, axis=1, keepdims=True)
    )
    dispatch_grad = dot("md,sd->ms", tokens, slot_in_grad)
    logit_grad = (dispatch * (dispatch_grad - slot_stat[None]) + combine_logit).astype(BF)
    d_tokens = (
        dot("ms,ds->md", logit_grad, router) + dot("ms,sd->md", dispatch_cast, slot_in_grad)
    ).astype(BF)
    term = dot("ms,md->sd", logit_grad, tokens)
    term = jnp.sum(exchange(term.reshape(16, 4, 1280), RING), axis=0)
    term = jnp.broadcast_to(term.astype(BF)[None], (32, 4, 1280))
    term = jnp.sum(exchange(term, REST).astype(F32), axis=0).astype(BF)
    term = exchange(jnp.broadcast_to(term[None], (16, 4, 1280)), RING)
    d_router = term.reshape(32, 2, 1280).transpose(2, 1, 0).reshape(1280, 64)
    d_kept = jnp.where(first, d_weight[:320], d_weight[320:])
    d_got = swap(jnp.where(first, d_weight[320:], d_weight[:320]))
    d_w_in = jnp.where(first, d_kept, d_got)
    d_w_out = jnp.where(first, d_got, d_kept)
    return (d_tokens[None], d_router, d_w_in[None], d_w_out[None])


def solution(mesh):
    fine = Mesh(
        mesh.devices.reshape(4, 2, 2, 4, 8), ("y_lo", "core", "y_hi", "x", "z")
    )
    image = P(DP + EXPERT, None, None)
    unit = P(EXPERT, DP, None)
    return jax.shard_map(
        local,
        mesh=fine,
        in_specs=(image, image, P(), unit, unit),
        out_specs=(image, P(), unit, unit),
        check_vma=False,
    )
```

```python
import jax
import jax.numpy as jnp
from jax import lax
from jax.sharding import Mesh, PartitionSpec as P

SWAP = [(0, 1), (1, 0)]
DP = ("y_lo", "core")
EXPERT = ("y_hi", "x", "z")
CHIPS = ("y_lo",) + EXPERT
BF = jnp.bfloat16
F32 = jnp.float32


def gelu_back(preact, upstream):
    return jax.vjp(jax.nn.gelu, preact)[1](upstream)[0]


def exchange(blocks):
    return lax.all_to_all(blocks, CHIPS, split_axis=0, concat_axis=0, tiled=True)


def swap(value):
    return lax.ppermute(value, "core", SWAP)


def dot(spec, left, right):
    return jnp.einsum(spec, left, right, preferred_element_type=F32)


def local(tokens, grad_out, router, w_in, w_out):
    tokens, grad_out, w_in, w_out = tokens[0], grad_out[0], w_in[0], w_out[0]
    first = lax.axis_index("core") == 0
    weight_kept = jnp.where(first, w_in, w_out)
    weight_got = swap(jnp.where(first, w_out, w_in))
    weight = jnp.concatenate(
        [jnp.where(first, weight_kept, weight_got), jnp.where(first, weight_got, weight_kept)]
    )
    logits = dot("md,ds->ms", tokens, router)
    dispatch = jax.nn.softmax(logits, axis=0)
    combine = jax.nn.softmax(logits, axis=1)
    dispatch_cast = dispatch.astype(BF)
    own_in = dot("ms,md->sd", dispatch_cast, tokens).astype(BF)
    own_grad = dot("ms,md->sd", combine.astype(BF), grad_out).astype(BF)
    got = swap(jnp.where(first, own_grad, own_in))
    pair = jnp.stack(
        [jnp.where(first, own_in, got), jnp.where(first, got, own_grad)], axis=1
    )
    blocks = jnp.broadcast_to(pair[None], (4, 64, 2, 1280)).reshape(256, 2, 1280)
    rows = exchange(blocks).reshape(512, 1280)
    act = dot("id,hd->ih", rows, weight)
    other = swap(jnp.where(first, jax.nn.gelu(act), act).astype(BF))
    hid = jnp.where(first, gelu_back(act, other.astype(F32)).astype(BF), other)
    partial = dot("ih,hd->id", hid, weight).astype(BF)
    d_weight = dot("ih,id->hd", hid, rows).astype(BF)
    parts = exchange(partial.reshape(256, 2, 1280)).reshape(4, 64, 2, 1280)
    back = jnp.sum(parts.astype(F32), axis=0).astype(BF)
    kept = jnp.where(first, back[:, 0], back[:, 1])
    got = swap(jnp.where(first, back[:, 1], back[:, 0]))
    slot_in_grad = jnp.where(first, kept, got)
    slot_out = jnp.where(first, got, kept)
    slot_stat = jnp.sum(own_in.astype(F32) * slot_in_grad.astype(F32), axis=1)
    combine_grad = dot("md,sd->ms", grad_out, slot_out)
    combine_logit = combine * (
        combine_grad - jnp.sum(combine * combine_grad, axis=1, keepdims=True)
    )
    dispatch_grad = dot("md,sd->ms", tokens, slot_in_grad)
    logit_grad = (dispatch * (dispatch_grad - slot_stat[None]) + combine_logit).astype(BF)
    d_tokens = (
        dot("ms,ds->md", logit_grad, router) + dot("ms,sd->md", dispatch_cast, slot_in_grad)
    ).astype(BF)
    term = dot("ms,md->sd", logit_grad, tokens)
    half = jnp.where(first, term[:32], term[32:]) + swap(jnp.where(first, term[32:], term[:32]))
    half = half.reshape(32, 5, 2, 128).swapaxes(0, 1).reshape(160, 2, 128)
    half = jnp.concatenate([half, jnp.zeros((96, 2, 128), F32)])
    piece = jnp.sum(exchange(half), axis=0).astype(BF)
    pieces = exchange(jnp.broadcast_to(piece[None], (256, 2, 128)))
    half = pieces[:160].reshape(5, 32, 2, 128).swapaxes(0, 1).reshape(32, 1280)
    got = swap(half)
    d_router = jnp.concatenate([jnp.where(first, half, got), jnp.where(first, got, half)]).T
    d_kept = jnp.where(first, d_weight[:320], d_weight[320:])
    d_got = swap(jnp.where(first, d_weight[320:], d_weight[:320]))
    d_w_in = jnp.where(first, d_kept, d_got)
    d_w_out = jnp.where(first, d_got, d_kept)
    return (d_tokens[None], d_router, d_w_in[None], d_w_out[None])


def solution(mesh):
    fine = Mesh(
        mesh.devices.reshape(4, 2, 2, 4, 8), ("y_lo", "core", "y_hi", "x", "z")
    )
    image = P(DP + EXPERT, None, None)
    unit = P(EXPERT, DP, None)
    return jax.shard_map(
        local,
        mesh=fine,
        in_specs=(image, image, P(), unit, unit),
        out_specs=(image, P(), unit, unit),
        check_vma=False,
    )
```

```python
import jax
import jax.numpy as jnp
from jax import lax
from jax.sharding import Mesh, PartitionSpec as P

SWAP = [(0, 1), (1, 0)]
DP = ("y_lo", "core")
EXPERT = ("y_hi", "x", "z")
CHIPS = ("y_lo",) + EXPERT
BF = jnp.bfloat16
F32 = jnp.float32


def gelu_back(preact, upstream):
    return jax.vjp(jax.nn.gelu, preact)[1](upstream)[0]


def exchange(blocks):
    return lax.all_to_all(blocks, CHIPS, split_axis=0, concat_axis=0, tiled=True)


def swap(value):
    return lax.ppermute(value, "core", SWAP)


def dot(spec, left, right):
    return jnp.einsum(spec, left, right, preferred_element_type=F32)


def local(tokens, grad_out, router, w_in, w_out):
    tokens, grad_out, w_in, w_out = tokens[0], grad_out[0], w_in[0], w_out[0]
    first = lax.axis_index("core") == 0
    weight_kept = jnp.where(first, w_in, w_out)
    weight_got = swap(jnp.where(first, w_out, w_in))
    weight = jnp.concatenate(
        [jnp.where(first, weight_kept, weight_got), jnp.where(first, weight_got, weight_kept)]
    )
    logits = dot("md,ds->ms", tokens, router)
    dispatch = jax.nn.softmax(logits, axis=0)
    combine = jax.nn.softmax(logits, axis=1)
    dispatch_cast = dispatch.astype(BF)
    own_in = dot("ms,md->sd", dispatch_cast, tokens).astype(BF)
    own_grad = dot("ms,md->sd", combine.astype(BF), grad_out).astype(BF)
    got = swap(jnp.where(first, own_grad, own_in))
    pair = jnp.stack(
        [jnp.where(first, own_in, got), jnp.where(first, got, own_grad)], axis=1
    )
    blocks = jnp.broadcast_to(pair[None], (4, 64, 2, 1280)).reshape(256, 2, 1280)
    rows = exchange(blocks).reshape(512, 1280)
    act = dot("id,hd->ih", rows, weight)
    other = swap(jnp.where(first, jax.nn.gelu(act), act).astype(BF))
    hid = jnp.where(first, gelu_back(act, other.astype(F32)).astype(BF), other)
    partial = dot("ih,hd->id", hid, weight).astype(BF)
    d_weight = dot("ih,id->hd", hid, rows).astype(BF)
    parts = exchange(partial.reshape(256, 2, 1280)).reshape(4, 64, 2, 1280)
    d_kept = jnp.where(first, d_weight[:320], d_weight[320:])
    d_got = swap(jnp.where(first, d_weight[320:], d_weight[:320]))
    parts, d_kept, d_got = lax.optimization_barrier((parts, d_kept, d_got))
    back = jnp.sum(parts.astype(F32), axis=0).astype(BF)
    kept = jnp.where(first, back[:, 0], back[:, 1])
    got = swap(jnp.where(first, back[:, 1], back[:, 0]))
    slot_in_grad = jnp.where(first, kept, got)
    slot_out = jnp.where(first, got, kept)
    slot_stat = jnp.sum(own_in.astype(F32) * slot_in_grad.astype(F32), axis=1)
    combine_grad = dot("md,sd->ms", grad_out, slot_out)
    combine_logit = combine * (
        combine_grad - jnp.sum(combine * combine_grad, axis=1, keepdims=True)
    )
    dispatch_grad = dot("md,sd->ms", tokens, slot_in_grad)
    logit_grad = (dispatch * (dispatch_grad - slot_stat[None]) + combine_logit).astype(BF)
    d_tokens = (
        dot("ms,ds->md", logit_grad, router) + dot("ms,sd->md", dispatch_cast, slot_in_grad)
    ).astype(BF)
    term = dot("ms,md->sd", logit_grad, tokens).astype(BF)
    term = term.reshape(16, 4, 10, 128).swapaxes(1, 2).reshape(160, 4, 128)
    term = jnp.concatenate([term, jnp.zeros((96, 4, 128), BF)])
    piece = jnp.sum(exchange(term).astype(F32), axis=0).astype(BF)
    pieces = exchange(jnp.broadcast_to(piece[None], (256, 4, 128)))
    total = pieces[:160].reshape(16, 10, 4, 128).swapaxes(1, 2).reshape(64, 1280)
    d_router = (total.astype(F32) + swap(total).astype(F32)).astype(BF).T
    d_w_in = jnp.where(first, d_kept, d_got)
    d_w_out = jnp.where(first, d_got, d_kept)
    return (d_tokens[None], d_router, d_w_in[None], d_w_out[None])


def solution(mesh):
    fine = Mesh(
        mesh.devices.reshape(4, 2, 2, 4, 8), ("y_lo", "core", "y_hi", "x", "z")
    )
    image = P(DP + EXPERT, None, None)
    unit = P(EXPERT, DP, None)
    return jax.shard_map(
        local,
        mesh=fine,
        in_specs=(image, image, P(), unit, unit),
        out_specs=(image, P(), unit, unit),
        check_vma=False,
    )
```

```python
import jax
import jax.numpy as jnp
from jax import lax
from jax.sharding import Mesh, PartitionSpec as P

SWAP = [(0, 1), (1, 0)]
DP = ("y_lo", "core")
EXPERT = ("y_hi", "x", "z")
CHIPS = ("y_lo",) + EXPERT
PLANE = ("x", "z")
LINE = ("y_lo", "core", "y_hi")
BF = jnp.bfloat16
F32 = jnp.float32


def gelu_back(preact, upstream):
    return jax.vjp(jax.nn.gelu, preact)[1](upstream)[0]


def exchange(blocks, axes):
    return lax.all_to_all(blocks, axes, split_axis=0, concat_axis=0, tiled=True)


def swap(value):
    return lax.ppermute(value, "core", SWAP)


def dot(spec, left, right):
    return jnp.einsum(spec, left, right, preferred_element_type=F32)


def local(tokens, grad_out, router, w_in, w_out):
    tokens, grad_out, w_in, w_out = tokens[0], grad_out[0], w_in[0], w_out[0]
    first = lax.axis_index("core") == 0
    weight_kept = jnp.where(first, w_in, w_out)
    weight_got = swap(jnp.where(first, w_out, w_in))
    weight = jnp.concatenate(
        [jnp.where(first, weight_kept, weight_got), jnp.where(first, weight_got, weight_kept)]
    )
    logits = dot("md,ds->ms", tokens, router)
    dispatch = jax.nn.softmax(logits, axis=0)
    combine = jax.nn.softmax(logits, axis=1)
    dispatch_cast = dispatch.astype(BF)
    own_in = dot("ms,md->sd", dispatch_cast, tokens).astype(BF)
    own_grad = dot("ms,md->sd", combine.astype(BF), grad_out).astype(BF)
    got = swap(jnp.where(first, own_grad, own_in))
    pair = jnp.stack(
        [jnp.where(first, own_in, got), jnp.where(first, got, own_grad)], axis=1
    )
    blocks = jnp.broadcast_to(pair[None], (4, 64, 2, 1280)).reshape(256, 2, 1280)
    rows = exchange(blocks, CHIPS).reshape(512, 1280)
    act = dot("id,hd->ih", rows, weight)
    other = swap(jnp.where(first, jax.nn.gelu(act), act).astype(BF))
    hid = jnp.where(first, gelu_back(act, other.astype(F32)).astype(BF), other)
    partial = dot("ih,hd->id", hid, weight).astype(BF)
    d_weight = dot("ih,id->hd", hid, rows).astype(BF)
    parts = exchange(partial.reshape(256, 2, 1280), CHIPS).reshape(512, 1280)
    d_kept = jnp.where(first, d_weight[:320], d_weight[320:])
    d_got = swap(jnp.where(first, d_weight[320:], d_weight[:320]))
    parts, d_kept, d_got = lax.optimization_barrier((parts, d_kept, d_got))
    row = lax.broadcasted_iota(jnp.int32, (128, 512), 0)
    col = lax.broadcasted_iota(jnp.int32, (128, 512), 1)
    image = jnp.where(first, row // 64, 1 - row // 64)
    adder = (col % 128 == (row % 64) * 2 + image).astype(BF)
    back = dot("sr,rd->sd", adder, parts).astype(BF)
    kept = back[:64]
    got = swap(back[64:])
    slot_in_grad = jnp.where(first, kept, got)
    slot_out = jnp.where(first, got, kept)
    slot_stat = jnp.sum(own_in.astype(F32) * slot_in_grad.astype(F32), axis=1)
    combine_grad = dot("md,sd->ms", grad_out, slot_out)
    combine_logit = combine * (
        combine_grad - jnp.sum(combine * combine_grad, axis=1, keepdims=True)
    )
    dispatch_grad = dot("md,sd->ms", tokens, slot_in_grad)
    logit_grad = (dispatch * (dispatch_grad - slot_stat[None]) + combine_logit).astype(BF)
    d_tokens = (
        dot("ms,ds->md", logit_grad, router) + dot("ms,sd->md", dispatch_cast, slot_in_grad)
    ).astype(BF)
    term = dot("ms,md->sd", logit_grad, tokens).astype(BF)
    term = jnp.sum(exchange(term.reshape(32, 2, 1280), PLANE).astype(F32), axis=0).astype(BF)
    term = exchange(jnp.broadcast_to(term[None], (16, 2, 1280)), LINE)
    term = jnp.sum(term.astype(F32), axis=0).astype(BF)
    term = exchange(jnp.broadcast_to(term[None], (32, 2, 1280)), PLANE)
    d_router = term.reshape(64, 1280).T
    d_w_in = jnp.where(first, d_kept, d_got)
    d_w_out = jnp.where(first, d_got, d_kept)
    return (d_tokens[None], d_router, d_w_in[None], d_w_out[None])


def solution(mesh):
    fine = Mesh(
        mesh.devices.reshape(4, 2, 2, 4, 8), ("y_lo", "core", "y_hi", "x", "z")
    )
    image = P(DP + EXPERT, None, None)
    unit = P(EXPERT, DP, None)
    return jax.shard_map(
        local,
        mesh=fine,
        in_specs=(image, image, P(), unit, unit),
        out_specs=(image, P(), unit, unit),
        check_vma=False,
    )
```

```python
import math

import jax
import jax.numpy as jnp
from jax import lax
from jax.experimental import pallas as pl
from jax.experimental.pallas import tpu as pltpu
from jax.sharding import Mesh, PartitionSpec as P

SWAP = [(0, 1), (1, 0)]
DP = ("y_lo", "core")
EXPERT = ("y_hi", "x", "z")
CHIPS = ("y_lo",) + EXPERT
PLANE = ("x", "z")
LINE = ("y_lo", "core", "y_hi")
BF = jnp.bfloat16
F32 = jnp.float32


VMEM = pl.BlockSpec(memory_space=pltpu.VMEM)
HBM = pl.BlockSpec(memory_space=pltpu.HBM)
STEP = 128
GELU_A = math.sqrt(2.0 / math.pi)
GELU_B = 0.044715


def on_core(kernel, outs, out_specs, scratch=()):
    def call(*args):
        return pl.pallas_call(
            kernel,
            out_shape=outs,
            in_specs=[VMEM] * len(args),
            out_specs=out_specs,
            scratch_shapes=list(scratch),
            compiler_params=pltpu.CompilerParams(vmem_limit_bytes=32 * 2**20),
        )(*args)

    return call


def shape(*dims, dtype=BF):
    return jax.ShapeDtypeStruct(dims, dtype)


def spread_kernel(kept_ref, got_ref, out_ref, pair, sems):
    core = lax.axis_index("core")
    row = lax.broadcasted_iota(jnp.int32, (128, 64), 0)
    col = lax.broadcasted_iota(jnp.int32, (128, 64), 1)
    own = (row == 2 * col + core).astype(BF)
    other = (row == 2 * col + 1 - core).astype(BF)
    rows = jnp.dot(own, kept_ref[...], preferred_element_type=F32) + jnp.dot(
        other, got_ref[...], preferred_element_type=F32
    )
    pair.reshape(128, 1280)[...] = rows.astype(BF)
    copies = [pltpu.make_async_copy(pair, out_ref.at[i], sems.at[i]) for i in range(4)]
    for copy in copies:
        copy.start()
    for copy in copies:
        copy.wait()


def enter_kernel(blocks_ref, weight_ref, slope_ref, send_ref):
    first = lax.axis_index("core") == 0
    blocks = blocks_ref.reshape(512, 1280)
    for at in range(0, 512, STEP):
        part = pl.ds(at, STEP)
        v = lax.dot_general(
            blocks[part], weight_ref[...], (((1,), (1,)), ((), ())), preferred_element_type=F32
        )
        square = v * v
        t = jnp.tanh(GELU_A * v * (1.0 + GELU_B * square))
        half = 0.5 * (1.0 + t)
        send_ref[part] = jnp.where(first, v * half, v).astype(BF)
        slope_ref[part] = half + (0.5 * GELU_A) * v * (1.0 - t * t) * (
            1.0 + (3.0 * GELU_B) * square
        )


def leave_kernel(slope_ref, other_ref, weight_ref, hid_ref, out_ref, hids, blocks, hid_sems, sems):
    first = lax.axis_index("core") == 0
    copies = []
    for i in range(512 // STEP):
        part = pl.ds(i * STEP, STEP)
        other = other_ref[part].astype(F32)
        hid = jnp.where(first, slope_ref[part] * other, other).astype(BF)
        hids[part] = hid
        copies.append(pltpu.make_async_copy(hids.at[part], hid_ref.at[part], hid_sems.at[i]))
        copies[-1].start()
        rows = jnp.dot(hid, weight_ref[...], preferred_element_type=F32)
        blocks.reshape(512, 1280)[part] = rows.astype(BF)
        half = pl.ds(i * STEP // 2, STEP // 2)
        copies.append(pltpu.make_async_copy(blocks.at[half], out_ref.at[half], sems.at[i]))
        copies[-1].start()
    for copy in copies:
        copy.wait()


def add_kernel(parts_ref, kept_ref, send_ref):
    core = lax.axis_index("core")
    row = lax.broadcasted_iota(jnp.int32, (64, 512), 0)
    col = lax.broadcasted_iota(jnp.int32, (64, 512), 1) & 127
    parts = parts_ref.reshape(512, 1280)[...]
    for out_ref, image in ((kept_ref, core), (send_ref, 1 - core)):
        adder = (col == 2 * row + image).astype(BF)
        out_ref[...] = jnp.dot(adder, parts, preferred_element_type=F32).astype(BF)


spread = on_core(
    spread_kernel,
    shape(4, 64, 2, 1280),
    HBM,
    (pltpu.VMEM((64, 2, 1280), BF), pltpu.SemaphoreType.DMA((4,))),
)
enter = on_core(
    enter_kernel,
    (shape(512, 640, dtype=F32), shape(512, 640)),
    (VMEM, VMEM),
)
leave = on_core(
    leave_kernel,
    (shape(512, 640), shape(256, 2, 1280)),
    (HBM, HBM),
    (
        pltpu.VMEM((512, 640), BF),
        pltpu.VMEM((256, 2, 1280), BF),
        pltpu.SemaphoreType.DMA((512 // STEP,)),
        pltpu.SemaphoreType.DMA((512 // STEP,)),
    ),
)
add4 = on_core(add_kernel, (shape(64, 1280), shape(64, 1280)), (VMEM, VMEM))


def exchange(blocks, axes):
    return lax.all_to_all(blocks, axes, split_axis=0, concat_axis=0, tiled=True)


def swap(value):
    return lax.ppermute(value, "core", SWAP)


def dot(spec, left, right):
    return jnp.einsum(spec, left, right, preferred_element_type=F32)


def local(tokens, grad_out, router, w_in, w_out):
    tokens, grad_out, w_in, w_out = tokens[0], grad_out[0], w_in[0], w_out[0]
    first = lax.axis_index("core") == 0
    weight_kept = jnp.where(first, w_in, w_out)
    weight_got = swap(jnp.where(first, w_out, w_in))
    weight = jnp.concatenate(
        [jnp.where(first, weight_kept, weight_got), jnp.where(first, weight_got, weight_kept)]
    )
    logits = dot("md,ds->ms", tokens, router)
    dispatch = jax.nn.softmax(logits, axis=0)
    combine = jax.nn.softmax(logits, axis=1)
    dispatch_cast = dispatch.astype(BF)
    own_in = dot("ms,md->sd", dispatch_cast, tokens).astype(BF)
    own_grad = dot("ms,md->sd", combine.astype(BF), grad_out).astype(BF)
    kept = jnp.where(first, own_in, own_grad)
    got = swap(jnp.where(first, own_grad, own_in))
    blocks = exchange(spread(kept, got).reshape(256, 2, 1280), CHIPS)
    slope, send = enter(blocks, weight)
    hid, partial = leave(slope, swap(send), weight)
    d_weight = dot("ih,id->hd", hid, blocks.reshape(512, 1280)).astype(BF)
    parts = exchange(partial, CHIPS)
    d_kept = jnp.where(first, d_weight[:320], d_weight[320:])
    d_got = swap(jnp.where(first, d_weight[320:], d_weight[:320]))
    parts, d_kept, d_got = lax.optimization_barrier((parts, d_kept, d_got))
    kept, send = add4(parts)
    got = swap(send)
    slot_in_grad = jnp.where(first, kept, got)
    slot_out = jnp.where(first, got, kept)
    slot_stat = jnp.sum(own_in.astype(F32) * slot_in_grad.astype(F32), axis=1)
    combine_grad = dot("md,sd->ms", grad_out, slot_out)
    combine_logit = combine * (
        combine_grad - jnp.sum(combine * combine_grad, axis=1, keepdims=True)
    )
    dispatch_grad = dot("md,sd->ms", tokens, slot_in_grad)
    logit_grad = (dispatch * (dispatch_grad - slot_stat[None]) + combine_logit).astype(BF)
    d_tokens = (
        dot("ms,ds->md", logit_grad, router) + dot("ms,sd->md", dispatch_cast, slot_in_grad)
    ).astype(BF)
    term = dot("ms,md->sd", logit_grad, tokens).astype(BF)
    term = jnp.sum(exchange(term.reshape(32, 2, 1280), PLANE).astype(F32), axis=0).astype(BF)
    term = exchange(jnp.broadcast_to(term[None], (16, 2, 1280)), LINE)
    term = jnp.sum(term.astype(F32), axis=0).astype(BF)
    term = exchange(jnp.broadcast_to(term[None], (32, 2, 1280)), PLANE)
    d_router = term.reshape(64, 1280).T
    d_w_in = jnp.where(first, d_kept, d_got)
    d_w_out = jnp.where(first, d_got, d_kept)
    return (d_tokens[None], d_router, d_w_in[None], d_w_out[None])


def solution(mesh):
    fine = Mesh(
        mesh.devices.reshape(4, 2, 2, 4, 8), ("y_lo", "core", "y_hi", "x", "z")
    )
    image = P(DP + EXPERT, None, None)
    unit = P(EXPERT, DP, None)
    return jax.shard_map(
        local,
        mesh=fine,
        in_specs=(image, image, P(), unit, unit),
        out_specs=(image, P(), unit, unit),
        check_vma=False,
    )
```

```python
import math

import jax
import jax.numpy as jnp
from jax import lax
from jax.experimental import pallas as pl
from jax.experimental.pallas import tpu as pltpu
from jax.sharding import Mesh, PartitionSpec as P

SWAP = [(0, 1), (1, 0)]
DP = ("y_lo", "core")
EXPERT = ("y_hi", "x", "z")
CHIPS = ("y_lo",) + EXPERT
PLANE = ("x", "z")
LINE = ("y_lo", "core", "y_hi")
BF = jnp.bfloat16
F32 = jnp.float32


VMEM = pl.BlockSpec(memory_space=pltpu.VMEM)
HBM = pl.BlockSpec(memory_space=pltpu.HBM)
STEP = 128
GELU_A = math.sqrt(2.0 / math.pi)
GELU_B = 0.044715


def dot_last(left, right):
    return lax.dot_general(
        left, right, (((1,), (1,)), ((), ())), preferred_element_type=F32
    )


def dot_first(left, right):
    return lax.dot_general(
        left, right, (((0,), (0,)), ((), ())), preferred_element_type=F32
    )


def on_core(kernel, outs, out_specs, scratch=(), in_specs=None, aliases=None, grant=32 * 2**20):
    def call(*args):
        return pl.pallas_call(
            kernel,
            out_shape=outs,
            in_specs=[(in_specs or {}).get(i, VMEM) for i in range(len(args))],
            out_specs=out_specs,
            scratch_shapes=list(scratch),
            input_output_aliases=aliases or {},
            compiler_params=pltpu.CompilerParams(vmem_limit_bytes=grant),
        )(*args)

    return call


def shape(*dims, dtype=BF):
    return jax.ShapeDtypeStruct(dims, dtype)


def spread_kernel(kept_ref, got_ref, out_ref, pair, sems):
    core = lax.axis_index("core")
    row = lax.broadcasted_iota(jnp.int32, (128, 64), 0)
    col = lax.broadcasted_iota(jnp.int32, (128, 64), 1)
    own = (row == 2 * col + core).astype(BF)
    other = (row == 2 * col + 1 - core).astype(BF)
    rows = jnp.dot(own, kept_ref[...], preferred_element_type=F32) + jnp.dot(
        other, got_ref[...], preferred_element_type=F32
    )
    pair.reshape(128, 1280)[...] = rows.astype(BF)
    copies = [pltpu.make_async_copy(pair, out_ref.at[i], sems.at[i]) for i in range(4)]
    for copy in copies:
        copy.start()
    for copy in copies:
        copy.wait()


def enter_kernel(blocks_ref, weight_ref, slope_ref, send_ref):
    first = lax.axis_index("core") == 0
    blocks = blocks_ref.reshape(512, 1280)
    for at in range(0, 512, STEP):
        part = pl.ds(at, STEP)
        v = dot_last(blocks[part], weight_ref[...])
        square = v * v
        t = jnp.tanh(GELU_A * v * (1.0 + GELU_B * square))
        half = 0.5 * (1.0 + t)
        send_ref[part] = jnp.where(first, v * half, v).astype(BF)
        slope_ref[part] = half + (0.5 * GELU_A) * v * (1.0 - t * t) * (
            1.0 + (3.0 * GELU_B) * square
        )


def leave_kernel(
    slope_ref, other_ref, weight_ref, spent_ref, out_ref, hid_ref, blocks, hids, sems
):
    del spent_ref
    first = lax.axis_index("core") == 0
    copies = []
    for i in range(512 // STEP):
        part = pl.ds(i * STEP, STEP)
        other = other_ref[part].astype(F32)
        hid = jnp.where(first, slope_ref[part] * other, other).astype(BF)
        hids[part] = hid
        copies.append(pltpu.make_async_copy(hids.at[part], hid_ref.at[part], sems.at[0, i]))
        copies[-1].start()
        rows = jnp.dot(hid, weight_ref[...], preferred_element_type=F32)
        blocks.reshape(512, 1280)[part] = rows.astype(BF)
        half = pl.ds(i * STEP // 2, STEP // 2)
        copies.append(pltpu.make_async_copy(blocks.at[half], out_ref.at[half], sems.at[1, i]))
        copies[-1].start()
    for copy in copies:
        copy.wait()


def image_kernel(
    tokens_ref, router_ref, grad_hbm, dispatch_ref, combine_ref, own_ref, kept_ref, send_ref, grad, sem
):
    copy = pltpu.make_async_copy(grad_hbm, grad, sem)
    copy.start()
    first = lax.axis_index("core") == 0
    tokens = tokens_ref[...]
    logits = dot_last(tokens, router_ref[...])
    dispatch = jnp.exp(logits - jnp.max(logits, axis=0, keepdims=True))
    dispatch = dispatch / jnp.sum(dispatch, axis=0, keepdims=True)
    dispatch_ref[...] = dispatch
    own_in = dot_first(dispatch.astype(BF), tokens).astype(BF)
    own_ref[...] = own_in
    combine = jnp.exp(logits - jnp.max(logits, axis=1, keepdims=True))
    combine = combine / jnp.sum(combine, axis=1, keepdims=True)
    combine_ref[...] = combine
    copy.wait()
    own_grad = dot_first(combine.astype(BF), grad[...]).astype(BF)
    kept_ref[...] = jnp.where(first, own_in, own_grad)
    send_ref[...] = jnp.where(first, own_grad, own_in)


def logit_kernel(
    tokens_ref, grad_hbm, dispatch_ref, combine_ref, own_ref, kept_ref, got_ref,
    slot_ref, logit_ref, term_ref, grad, sem,
):
    copy = pltpu.make_async_copy(grad_hbm, grad, sem)
    copy.start()
    first = lax.axis_index("core") == 0
    tokens = tokens_ref[...]
    kept, got = kept_ref[...], got_ref[...]
    slot_in_grad = jnp.where(first, kept, got)
    slot_out = jnp.where(first, got, kept)
    slot_ref[...] = slot_in_grad
    row = lax.broadcasted_iota(jnp.int32, (64, 64), 0)
    col = lax.broadcasted_iota(jnp.int32, (64, 64), 1)
    stat = jnp.sum(
        jnp.where(row == col, dot_last(own_ref[...], slot_in_grad), 0.0), axis=0, keepdims=True
    )
    slot_part = dispatch_ref[...] * (dot_last(tokens, slot_in_grad) - stat)
    copy.wait()
    combine = combine_ref[...]
    combine_grad = dot_last(grad[...], slot_out)
    mean = jnp.sum(combine * combine_grad, axis=1, keepdims=True)
    logit_grad = (slot_part + combine * (combine_grad - mean)).astype(BF)
    logit_ref[...] = logit_grad
    term_ref.reshape(64, 1280)[...] = dot_first(logit_grad, tokens).astype(BF)


def add_kernel(parts_ref, kept_ref, send_ref):
    core = lax.axis_index("core")
    row = lax.broadcasted_iota(jnp.int32, (64, 512), 0)
    col = lax.broadcasted_iota(jnp.int32, (64, 512), 1) & 127
    parts = parts_ref.reshape(512, 1280)[...]
    for out_ref, image in ((kept_ref, core), (send_ref, 1 - core)):
        adder = (col == 2 * row + image).astype(BF)
        out_ref[...] = jnp.dot(adder, parts, preferred_element_type=F32).astype(BF)


spread = on_core(
    spread_kernel,
    shape(4, 64, 2, 1280),
    HBM,
    (pltpu.VMEM((64, 2, 1280), BF), pltpu.SemaphoreType.DMA((4,))),
)
enter = on_core(
    enter_kernel,
    (shape(512, 640, dtype=F32), shape(512, 640)),
    (VMEM, VMEM),
)
leave = on_core(
    leave_kernel,
    (shape(256, 2, 1280), shape(512, 640)),
    (HBM, HBM),
    (
        pltpu.VMEM((256, 2, 1280), BF),
        pltpu.VMEM((512, 640), BF),
        pltpu.SemaphoreType.DMA((2, 512 // STEP)),
    ),
    {3: HBM},
    {3: 0},
)
GRAD = (pltpu.VMEM((192, 1280), BF), pltpu.SemaphoreType.DMA(()))
enter_slots = on_core(
    image_kernel,
    (shape(192, 64, dtype=F32), shape(192, 64, dtype=F32)) + (shape(64, 1280),) * 3,
    (VMEM,) * 5,
    GRAD,
    {1: VMEM, 2: HBM},
    grant=63_000_000,
)
logits_back = on_core(
    logit_kernel,
    (shape(64, 1280), shape(192, 64), shape(32, 2, 1280)),
    (VMEM,) * 3,
    GRAD,
    {1: HBM},
)
add4 = on_core(add_kernel, (shape(64, 1280), shape(64, 1280)), (VMEM, VMEM))


def exchange(blocks, axes):
    return lax.all_to_all(blocks, axes, split_axis=0, concat_axis=0, tiled=True)


def swap(value):
    return lax.ppermute(value, "core", SWAP)


def dot(spec, left, right):
    return jnp.einsum(spec, left, right, preferred_element_type=F32)


def local(tokens, grad_out, router, w_in, w_out):
    tokens, grad_out, w_in, w_out = tokens[0], grad_out[0], w_in[0], w_out[0]
    first = lax.axis_index("core") == 0
    weight_kept = jnp.where(first, w_in, w_out)
    weight_got = swap(jnp.where(first, w_out, w_in))
    weight = jnp.concatenate(
        [jnp.where(first, weight_kept, weight_got), jnp.where(first, weight_got, weight_kept)]
    )
    dispatch, combine, own_in, kept, send = enter_slots(tokens, router.T, grad_out)
    spent = spread(kept, swap(send)).reshape(256, 2, 1280)
    blocks = exchange(spent, CHIPS)
    slope, send = enter(blocks, weight)
    partial, hid = leave(slope, swap(send), weight, spent)
    parts = exchange(partial, CHIPS)
    d_weight = dot("ih,id->hd", hid, blocks.reshape(512, 1280)).astype(BF)
    d_kept = jnp.where(first, d_weight[:320], d_weight[320:])
    d_got = swap(jnp.where(first, d_weight[320:], d_weight[:320]))
    parts, d_kept, d_got = lax.optimization_barrier((parts, d_kept, d_got))
    kept, send = add4(parts)
    slot_in_grad, logit_grad, term = logits_back(
        tokens, grad_out, dispatch, combine, own_in, kept, swap(send)
    )
    d_tokens = (
        dot("ms,ds->md", logit_grad, router)
        + dot("ms,sd->md", dispatch.astype(BF), slot_in_grad)
    ).astype(BF)
    term = jnp.sum(exchange(term, PLANE).astype(F32), axis=0).astype(BF)
    term = exchange(jnp.broadcast_to(term[None], (16, 2, 1280)), LINE)
    term = jnp.sum(term.astype(F32), axis=0).astype(BF)
    term = exchange(jnp.broadcast_to(term[None], (32, 2, 1280)), PLANE)
    d_router = term.reshape(64, 1280).T
    d_w_in = jnp.where(first, d_kept, d_got)
    d_w_out = jnp.where(first, d_got, d_kept)
    return (d_tokens[None], d_router, d_w_in[None], d_w_out[None])


def solution(mesh):
    fine = Mesh(
        mesh.devices.reshape(4, 2, 2, 4, 8), ("y_lo", "core", "y_hi", "x", "z")
    )
    image = P(DP + EXPERT, None, None)
    unit = P(EXPERT, DP, None)
    return jax.shard_map(
        local,
        mesh=fine,
        in_specs=(image, image, P(), unit, unit),
        out_specs=(image, P(), unit, unit),
        check_vma=False,
    )
```

```python
import math

import jax
import jax.numpy as jnp
from jax import lax
from jax.experimental import pallas as pl
from jax.experimental.pallas import tpu as pltpu
from jax.sharding import Mesh, PartitionSpec as P

SWAP = [(0, 1), (1, 0)]
DP = ("y_lo", "core")
EXPERT = ("y_hi", "x", "z")
CHIPS = ("y_lo",) + EXPERT
PLANE = ("x", "z")
LINE = ("y_lo", "core", "y_hi")
BF = jnp.bfloat16
F32 = jnp.float32


VMEM = pl.BlockSpec(memory_space=pltpu.VMEM)
HBM = pl.BlockSpec(memory_space=pltpu.HBM)
STEP = 128
GELU_A = math.sqrt(2.0 / math.pi)
GELU_B = 0.044715


def dot_last(left, right):
    return lax.dot_general(
        left, right, (((1,), (1,)), ((), ())), preferred_element_type=F32
    )


def dot_first(left, right):
    return lax.dot_general(
        left, right, (((0,), (0,)), ((), ())), preferred_element_type=F32
    )


def on_core(kernel, outs, out_specs, scratch=(), in_specs=None, aliases=None, grant=32 * 2**20):
    def call(*args):
        return pl.pallas_call(
            kernel,
            out_shape=outs,
            in_specs=[(in_specs or {}).get(i, VMEM) for i in range(len(args))],
            out_specs=out_specs,
            scratch_shapes=list(scratch),
            input_output_aliases=aliases or {},
            compiler_params=pltpu.CompilerParams(vmem_limit_bytes=grant),
        )(*args)

    return call


def shape(*dims, dtype=BF):
    return jax.ShapeDtypeStruct(dims, dtype)


def spread_kernel(kept_ref, got_ref, out_ref, pair, sems):
    core = lax.axis_index("core")
    row = lax.broadcasted_iota(jnp.int32, (128, 64), 0)
    col = lax.broadcasted_iota(jnp.int32, (128, 64), 1)
    own = (row == 2 * col + core).astype(BF)
    other = (row == 2 * col + 1 - core).astype(BF)
    rows = jnp.dot(own, kept_ref[...], preferred_element_type=F32) + jnp.dot(
        other, got_ref[...], preferred_element_type=F32
    )
    pair.reshape(128, 1280)[...] = rows.astype(BF)
    copies = [pltpu.make_async_copy(pair, out_ref.at[i], sems.at[i]) for i in range(4)]
    for copy in copies:
        copy.start()
    for copy in copies:
        copy.wait()


def enter_kernel(blocks_ref, weight_ref, slope_ref, send_ref):
    first = lax.axis_index("core") == 0
    blocks = blocks_ref.reshape(512, 1280)
    for at in range(0, 512, STEP):
        part = pl.ds(at, STEP)
        v = dot_last(blocks[part], weight_ref[...])
        square = v * v
        t = jnp.tanh(GELU_A * v * (1.0 + GELU_B * square))
        half = 0.5 * (1.0 + t)
        send_ref[part] = jnp.where(first, v * half, v).astype(BF)
        slope_ref[part] = half + (0.5 * GELU_A) * v * (1.0 - t * t) * (
            1.0 + (3.0 * GELU_B) * square
        )


def leave_kernel(
    slope_ref, other_ref, weight_ref, spent_ref, out_ref, hid_ref, blocks, hids, sems
):
    del spent_ref
    first = lax.axis_index("core") == 0
    copies = []
    for i in range(512 // STEP):
        part = pl.ds(i * STEP, STEP)
        other = other_ref[part].astype(F32)
        hid = jnp.where(first, slope_ref[part] * other, other).astype(BF)
        hids[part] = hid
        copies.append(pltpu.make_async_copy(hids.at[part], hid_ref.at[part], sems.at[0, i]))
        copies[-1].start()
        rows = jnp.dot(hid, weight_ref[...], preferred_element_type=F32)
        blocks.reshape(512, 1280)[part] = rows.astype(BF)
        half = pl.ds(i * STEP // 2, STEP // 2)
        copies.append(pltpu.make_async_copy(blocks.at[half], out_ref.at[half], sems.at[1, i]))
        copies[-1].start()
    for copy in copies:
        copy.wait()


def image_kernel(
    tokens_ref, router_ref, grad_hbm, dispatch_ref, combine_ref, own_ref, kept_ref, send_ref, grad, sem
):
    copy = pltpu.make_async_copy(grad_hbm, grad, sem)
    copy.start()
    first = lax.axis_index("core") == 0
    tokens = tokens_ref[...]
    logits = dot_last(tokens, router_ref[...])
    dispatch = jnp.exp(logits - jnp.max(logits, axis=0, keepdims=True))
    dispatch = dispatch / jnp.sum(dispatch, axis=0, keepdims=True)
    dispatch_ref[...] = dispatch
    own_in = dot_first(dispatch.astype(BF), tokens).astype(BF)
    own_ref[...] = own_in
    combine = jnp.exp(logits - jnp.max(logits, axis=1, keepdims=True))
    combine = combine / jnp.sum(combine, axis=1, keepdims=True)
    combine_ref[...] = combine
    copy.wait()
    own_grad = dot_first(combine.astype(BF), grad[...]).astype(BF)
    kept_ref[...] = jnp.where(first, own_in, own_grad)
    send_ref[...] = jnp.where(first, own_grad, own_in)


def logit_kernel(
    tokens_ref, grad_hbm, dispatch_ref, combine_ref, own_ref, kept_ref, got_ref,
    slot_ref, logit_ref, term_ref, grad, sem,
):
    copy = pltpu.make_async_copy(grad_hbm, grad, sem)
    copy.start()
    first = lax.axis_index("core") == 0
    tokens = tokens_ref[...]
    kept, got = kept_ref[...], got_ref[...]
    slot_in_grad = jnp.where(first, kept, got)
    slot_out = jnp.where(first, got, kept)
    slot_ref[...] = slot_in_grad
    row = lax.broadcasted_iota(jnp.int32, (64, 64), 0)
    col = lax.broadcasted_iota(jnp.int32, (64, 64), 1)
    stat = jnp.sum(
        jnp.where(row == col, dot_last(own_ref[...], slot_in_grad), 0.0), axis=0, keepdims=True
    )
    slot_part = dispatch_ref[...] * (dot_last(tokens, slot_in_grad) - stat)
    copy.wait()
    combine = combine_ref[...]
    combine_grad = dot_last(grad[...], slot_out)
    mean = jnp.sum(combine * combine_grad, axis=1, keepdims=True)
    logit_grad = (slot_part + combine * (combine_grad - mean)).astype(BF)
    logit_ref[...] = logit_grad
    term_ref.reshape(64, 1280)[...] = dot_first(logit_grad, tokens).astype(BF)


def add_kernel(parts_ref, kept_ref, send_ref):
    core = lax.axis_index("core")
    row = lax.broadcasted_iota(jnp.int32, (64, 512), 0)
    col = lax.broadcasted_iota(jnp.int32, (64, 512), 1) & 127
    parts = parts_ref.reshape(512, 1280)[...]
    for out_ref, image in ((kept_ref, core), (send_ref, 1 - core)):
        adder = (col == 2 * row + image).astype(BF)
        out_ref[...] = jnp.dot(adder, parts, preferred_element_type=F32).astype(BF)


spread = on_core(
    spread_kernel,
    shape(4, 64, 2, 1280),
    HBM,
    (pltpu.VMEM((64, 2, 1280), BF), pltpu.SemaphoreType.DMA((4,))),
)
enter = on_core(
    enter_kernel,
    (shape(512, 640, dtype=F32), shape(512, 640)),
    (VMEM, VMEM),
)
leave = on_core(
    leave_kernel,
    (shape(256, 2, 1280), shape(512, 640)),
    (HBM, HBM),
    (
        pltpu.VMEM((256, 2, 1280), BF),
        pltpu.VMEM((512, 640), BF),
        pltpu.SemaphoreType.DMA((2, 512 // STEP)),
    ),
    {3: HBM},
    {3: 0},
)
GRAD = (pltpu.VMEM((192, 1280), BF), pltpu.SemaphoreType.DMA(()))
enter_slots = on_core(
    image_kernel,
    (shape(192, 64, dtype=F32), shape(192, 64, dtype=F32)) + (shape(64, 1280),) * 3,
    (VMEM,) * 5,
    GRAD,
    {1: VMEM, 2: HBM},
    grant=63_000_000,
)
logits_back = on_core(
    logit_kernel,
    (shape(64, 1280), shape(192, 64), shape(32, 2, 1280)),
    (VMEM,) * 3,
    GRAD,
    {1: HBM},
)
add4 = on_core(add_kernel, (shape(64, 1280), shape(64, 1280)), (VMEM, VMEM))


def exchange(blocks, axes):
    return lax.all_to_all(blocks, axes, split_axis=0, concat_axis=0, tiled=True)


def swap(value):
    return lax.ppermute(value, "core", SWAP)


def dot(spec, left, right):
    return jnp.einsum(spec, left, right, preferred_element_type=F32)


def local(tokens, grad_out, router, w_in, w_out):
    tokens, grad_out, w_in, w_out = tokens[0], grad_out[0], w_in[0], w_out[0]
    first = lax.axis_index("core") == 0
    weight_kept = jnp.where(first, w_in, w_out)
    weight_got = swap(jnp.where(first, w_out, w_in))
    weight = jnp.concatenate(
        [jnp.where(first, weight_kept, weight_got), jnp.where(first, weight_got, weight_kept)]
    )
    dispatch, combine, own_in, kept, send = enter_slots(tokens, router.T, grad_out)
    spent = spread(kept, swap(send)).reshape(256, 2, 1280)
    blocks = exchange(spent, CHIPS)
    slope, send = enter(blocks, weight)
    partial, hid = leave(slope, swap(send), weight, spent)
    parts = exchange(partial, CHIPS)
    d_weight = dot("ih,id->hd", hid, blocks.reshape(512, 1280)).astype(BF)
    d_kept = jnp.where(first, d_weight[:320], d_weight[320:])
    d_got = swap(jnp.where(first, d_weight[320:], d_weight[:320]))
    d_w_in = jnp.where(first, d_kept, d_got)
    d_w_out = jnp.where(first, d_got, d_kept)
    parts, d_w_in, d_w_out = lax.optimization_barrier((parts, d_w_in, d_w_out))
    kept, send = add4(parts)
    slot_in_grad, logit_grad, term = logits_back(
        tokens, grad_out, dispatch, combine, own_in, kept, swap(send)
    )
    d_tokens = (
        dot("ms,ds->md", logit_grad, router)
        + dot("ms,sd->md", dispatch.astype(BF), slot_in_grad)
    ).astype(BF)
    term, d_tokens = lax.optimization_barrier((exchange(term, PLANE), d_tokens))
    term = jnp.sum(term.astype(F32), axis=0).astype(BF)
    term = exchange(jnp.broadcast_to(term[None], (16, 2, 1280)), LINE)
    term = jnp.sum(term.astype(F32), axis=0).astype(BF)
    term = exchange(jnp.broadcast_to(term[None], (32, 2, 1280)), PLANE)
    d_router = term.reshape(64, 1280).T
    return (d_tokens[None], d_router, d_w_in[None], d_w_out[None])


def solution(mesh):
    fine = Mesh(
        mesh.devices.reshape(4, 2, 2, 4, 8), ("y_lo", "core", "y_hi", "x", "z")
    )
    image = P(DP + EXPERT, None, None)
    unit = P(EXPERT, DP, None)
    return jax.shard_map(
        local,
        mesh=fine,
        in_specs=(image, image, P(), unit, unit),
        out_specs=(image, P(), unit, unit),
        check_vma=False,
    )
```

```python
import math

import jax
import jax.numpy as jnp
from jax import lax
from jax.experimental import pallas as pl
from jax.experimental.pallas import tpu as pltpu
from jax.sharding import Mesh, PartitionSpec as P

SWAP = [(0, 1), (1, 0)]
DP = ("y_lo", "core")
EXPERT = ("y_hi", "x", "z")
CHIPS = ("y_lo",) + EXPERT
PLANE = ("x", "z")
LINE = ("y_lo", "core", "y_hi")
BF = jnp.bfloat16
F32 = jnp.float32


VMEM = pl.BlockSpec(memory_space=pltpu.VMEM)
HBM = pl.BlockSpec(memory_space=pltpu.HBM)
STEP = 256
GELU_A = math.sqrt(2.0 / math.pi)
GELU_B = 0.044715


def dot_last(left, right):
    return lax.dot_general(
        left, right, (((1,), (1,)), ((), ())), preferred_element_type=F32
    )


def dot_first(left, right):
    return lax.dot_general(
        left, right, (((0,), (0,)), ((), ())), preferred_element_type=F32
    )


def on_core(kernel, outs, out_specs, scratch=(), in_specs=None, aliases=None, grant=32 * 2**20):
    def call(*args):
        return pl.pallas_call(
            kernel,
            out_shape=outs,
            in_specs=[(in_specs or {}).get(i, VMEM) for i in range(len(args))],
            out_specs=out_specs,
            scratch_shapes=list(scratch),
            input_output_aliases=aliases or {},
            compiler_params=pltpu.CompilerParams(vmem_limit_bytes=grant),
        )(*args)

    return call


def shape(*dims, dtype=BF):
    return jax.ShapeDtypeStruct(dims, dtype)


def image_kernel(
    tokens_ref, router_ref, grad_hbm, dispatch_ref, combine_ref, own_ref, out_ref, grad, pair, sems
):
    copy = pltpu.make_async_copy(grad_hbm, grad, sems.at[4])
    copy.start()
    tokens = tokens_ref[...]
    logits = dot_last(tokens, router_ref[...])
    dispatch = jnp.exp(logits - jnp.max(logits, axis=0, keepdims=True))
    dispatch = dispatch / jnp.sum(dispatch, axis=0, keepdims=True)
    dispatch_ref[...] = dispatch
    own_in = dot_first(dispatch.astype(BF), tokens).astype(BF)
    own_ref[...] = own_in
    pair[:, 0, :] = own_in
    combine = jnp.exp(logits - jnp.max(logits, axis=1, keepdims=True))
    combine = combine / jnp.sum(combine, axis=1, keepdims=True)
    combine_ref[...] = combine
    copy.wait()
    pair[:, 1, :] = dot_first(combine.astype(BF), grad[...]).astype(BF)
    copies = [pltpu.make_async_copy(pair, out_ref.at[i], sems.at[i]) for i in range(4)]
    for copy in copies:
        copy.start()
    for copy in copies:
        copy.wait()


def expert_kernel(
    blocks_ref, w_in_ref, w_out_hbm, spent_ref, hid_ref, grad_ref, out_ref, buffer, w_out_ref, sems
):
    del spent_ref
    load = pltpu.make_async_copy(w_out_hbm, w_out_ref, sems.at[256 // STEP])
    load.start()
    row = lax.broadcasted_iota(jnp.int32, (STEP, 2 * STEP), 0)
    col = lax.broadcasted_iota(jnp.int32, (STEP, 2 * STEP), 1)
    copies = []
    for i in range(256 // STEP):
        part = pl.ds(i * STEP, STEP)
        both = blocks_ref.reshape(512, 1280)[pl.ds(2 * i * STEP, 2 * STEP)]
        slot_in, slot_grad = (
            jnp.dot((col == 2 * row + kind).astype(BF), both, preferred_element_type=F32).astype(BF)
            for kind in (0, 1)
        )
        v = dot_last(slot_in, w_in_ref[...])
        if i == 0:
            load.wait()
        upstream = dot_last(slot_grad, w_out_ref[...])
        square = v * v
        t = jnp.tanh(GELU_A * v * (1.0 + GELU_B * square))
        half = 0.5 * (1.0 + t)
        slope = half + (0.5 * GELU_A) * v * (1.0 - t * t) * (1.0 + (3.0 * GELU_B) * square)
        hid = (v * half).astype(BF)
        grad = (slope * upstream).astype(BF)
        hid_ref[part] = hid
        grad_ref[part] = grad
        buffer[part, 0, :] = jnp.dot(
            hid, w_out_ref[...], preferred_element_type=F32
        ).astype(BF)
        buffer[part, 1, :] = jnp.dot(
            grad, w_in_ref[...], preferred_element_type=F32
        ).astype(BF)
        copies.append(pltpu.make_async_copy(buffer.at[part], out_ref.at[part], sems.at[i]))
        copies[-1].start()
    for copy in copies:
        copy.wait()


def logit_kernel(
    tokens_ref, grad_hbm, dispatch_ref, combine_ref, own_ref, parts_ref,
    slot_ref, logit_ref, term_ref, grad, sem,
):
    copy = pltpu.make_async_copy(grad_hbm, grad, sem)
    copy.start()
    tokens = tokens_ref[...]
    row = lax.broadcasted_iota(jnp.int32, (64, 512), 0)
    col = lax.broadcasted_iota(jnp.int32, (64, 512), 1) & 127
    parts = parts_ref.reshape(512, 1280)[...]
    slot_out, slot_in_grad = (
        jnp.dot((col == 2 * row + kind).astype(BF), parts, preferred_element_type=F32).astype(BF)
        for kind in (0, 1)
    )
    slot_ref[...] = slot_in_grad
    row = lax.broadcasted_iota(jnp.int32, (64, 64), 0)
    col = lax.broadcasted_iota(jnp.int32, (64, 64), 1)
    stat = jnp.sum(
        jnp.where(row == col, dot_last(own_ref[...], slot_in_grad), 0.0), axis=0, keepdims=True
    )
    slot_part = dispatch_ref[...] * (dot_last(tokens, slot_in_grad) - stat)
    copy.wait()
    combine = combine_ref[...]
    combine_grad = dot_last(grad[...], slot_out)
    mean = jnp.sum(combine * combine_grad, axis=1, keepdims=True)
    logit_grad = (slot_part + combine * (combine_grad - mean)).astype(BF)
    logit_ref[...] = logit_grad
    term_ref.reshape(64, 1280)[...] = dot_first(logit_grad, tokens).astype(BF)


image_slots = on_core(
    image_kernel,
    (
        shape(192, 64, dtype=F32),
        shape(192, 64, dtype=F32),
        shape(64, 1280),
        shape(4, 64, 2, 1280),
    ),
    (VMEM, VMEM, VMEM, HBM),
    (
        pltpu.VMEM((192, 1280), BF),
        pltpu.VMEM((64, 2, 1280), BF),
        pltpu.SemaphoreType.DMA((5,)),
    ),
    {2: HBM},
    grant=63_000_000,
)
experts = on_core(
    expert_kernel,
    (shape(256, 640), shape(256, 640), shape(256, 2, 1280)),
    (VMEM, VMEM, HBM),
    (
        pltpu.VMEM((256, 2, 1280), BF),
        pltpu.VMEM((640, 1280), BF),
        pltpu.SemaphoreType.DMA((256 // STEP + 1,)),
    ),
    {2: HBM, 3: HBM},
    {3: 2},
    grant=48 * 2**20,
)
logits_back = on_core(
    logit_kernel,
    (shape(64, 1280), shape(192, 64), shape(32, 2, 1280)),
    (VMEM,) * 3,
    (pltpu.VMEM((192, 1280), BF), pltpu.SemaphoreType.DMA(())),
    {1: HBM},
)


def exchange(blocks, axes):
    return lax.all_to_all(blocks, axes, split_axis=0, concat_axis=0, tiled=True)


def swap(value):
    return lax.ppermute(value, "core", SWAP)


def dot(spec, left, right):
    return jnp.einsum(spec, left, right, preferred_element_type=F32)


def local(tokens, grad_out, router, w_in, w_out):
    tokens, grad_out, w_in, w_out = tokens[0], grad_out[0], w_in[0], w_out[0]
    all_in = jnp.concatenate([w_in, swap(w_in)])
    all_out = jnp.concatenate([w_out, swap(w_out)])
    dispatch, combine, own_in, spent = image_slots(tokens, router.T, grad_out)
    spent = spent.reshape(256, 2, 1280)
    blocks = exchange(spent, CHIPS)
    hid, preact_grad, partial = experts(blocks, all_in, all_out, spent)
    parts = exchange(partial, CHIPS)
    d_in = dot("ih,id->hd", preact_grad, blocks[:, 0])
    d_out = dot("ih,id->hd", hid, blocks[:, 1])
    d_w_in = (d_in[:320] + swap(d_in[320:].astype(BF)).astype(F32)).astype(BF)
    d_w_out = (d_out[:320] + swap(d_out[320:].astype(BF)).astype(F32)).astype(BF)
    parts, d_w_in, d_w_out = lax.optimization_barrier((parts, d_w_in, d_w_out))
    slot_in_grad, logit_grad, term = logits_back(
        tokens, grad_out, dispatch, combine, own_in, parts
    )
    d_tokens = (
        dot("ms,ds->md", logit_grad, router)
        + dot("ms,sd->md", dispatch.astype(BF), slot_in_grad)
    ).astype(BF)
    term, d_tokens = lax.optimization_barrier((exchange(term, PLANE), d_tokens))
    term = jnp.sum(term.astype(F32), axis=0).astype(BF)
    term = exchange(jnp.broadcast_to(term[None], (16, 2, 1280)), LINE)
    term = jnp.sum(term.astype(F32), axis=0).astype(BF)
    term = exchange(jnp.broadcast_to(term[None], (32, 2, 1280)), PLANE)
    d_router = term.reshape(64, 1280).T
    return (d_tokens[None], d_router, d_w_in[None], d_w_out[None])


def solution(mesh):
    fine = Mesh(
        mesh.devices.reshape(4, 2, 2, 4, 8), ("y_lo", "core", "y_hi", "x", "z")
    )
    image = P(DP + EXPERT, None, None)
    unit = P(EXPERT, DP, None)
    return jax.shard_map(
        local,
        mesh=fine,
        in_specs=(image, image, P(), unit, unit),
        out_specs=(image, P(), unit, unit),
        check_vma=False,
    )
```

```python
import math

import jax
import jax.numpy as jnp
from jax import lax
from jax.experimental import pallas as pl
from jax.experimental.pallas import tpu as pltpu
from jax.sharding import Mesh, PartitionSpec as P

SWAP = [(0, 1), (1, 0)]
DP = ("y_lo", "core")
EXPERT = ("y_hi", "x", "z")
CHIPS = ("y_lo",) + EXPERT
PLANE = ("x", "z")
LINE = ("y_lo", "core", "y_hi")
BF = jnp.bfloat16
F32 = jnp.float32


VMEM = pl.BlockSpec(memory_space=pltpu.VMEM)
HBM = pl.BlockSpec(memory_space=pltpu.HBM)
GELU_A = math.sqrt(2.0 / math.pi)
GELU_B = 0.044715


def dot_last(left, right):
    return lax.dot_general(
        left, right, (((1,), (1,)), ((), ())), preferred_element_type=F32
    )


def dot_first(left, right):
    return lax.dot_general(
        left, right, (((0,), (0,)), ((), ())), preferred_element_type=F32
    )


def on_core(kernel, outs, out_specs, scratch=(), in_specs=None, aliases=None, grant=32 * 2**20):
    def call(*args):
        return pl.pallas_call(
            kernel,
            out_shape=outs,
            in_specs=[(in_specs or {}).get(i, VMEM) for i in range(len(args))],
            out_specs=out_specs,
            scratch_shapes=list(scratch),
            input_output_aliases=aliases or {},
            compiler_params=pltpu.CompilerParams(vmem_limit_bytes=grant),
        )(*args)

    return call


def shape(*dims, dtype=BF):
    return jax.ShapeDtypeStruct(dims, dtype)


def image_kernel(
    tokens_ref, router_ref, grad_hbm, dispatch_hbm, combine_hbm, own_hbm, out_ref,
    grad, dispatch_ref, combine_ref, own_ref, pair, sems,
):
    copy = pltpu.make_async_copy(grad_hbm, grad, sems.at[4])
    copy.start()
    tokens = tokens_ref[...]
    logits = dot_last(tokens, router_ref[...])
    dispatch = jnp.exp(logits - jnp.max(logits, axis=0, keepdims=True))
    dispatch = dispatch / jnp.sum(dispatch, axis=0, keepdims=True)
    dispatch_ref[...] = dispatch
    own_in = dot_first(dispatch.astype(BF), tokens).astype(BF)
    own_ref[...] = own_in
    copies = [
        pltpu.make_async_copy(dispatch_ref, dispatch_hbm, sems.at[5]),
        pltpu.make_async_copy(own_ref, own_hbm, sems.at[6]),
    ]
    for early in copies:
        early.start()
    pair[:, 0, :] = own_in
    combine = jnp.exp(logits - jnp.max(logits, axis=1, keepdims=True))
    combine = combine / jnp.sum(combine, axis=1, keepdims=True)
    combine_ref[...] = combine
    copies.append(pltpu.make_async_copy(combine_ref, combine_hbm, sems.at[7]))
    copies[-1].start()
    copy.wait()
    pair[:, 1, :] = dot_first(combine.astype(BF), grad[...]).astype(BF)
    late = [pltpu.make_async_copy(pair, out_ref.at[i], sems.at[i]) for i in range(4)]
    for each in late:
        each.start()
    for each in copies + late:
        each.wait()


def expert_kernel(
    blocks_ref, w_in_ref, w_out_hbm, spent_ref, hid_ref, grad_ref, out_ref, buffer, w_out_ref, sems
):
    del spent_ref
    load = pltpu.make_async_copy(w_out_hbm, w_out_ref, sems.at[0])
    load.start()
    row = lax.broadcasted_iota(jnp.int32, (128, 128), 0)
    col = lax.broadcasted_iota(jnp.int32, (128, 128), 1)
    sort = (col == 2 * (row & 63) + (row >> 6)).astype(BF)
    rows = blocks_ref.reshape(512, 1280)
    sorted_rows = [
        jnp.dot(sort, rows[pl.ds(at, 128)], preferred_element_type=F32).astype(BF)
        for at in range(0, 512, 128)
    ]
    v = dot_last(w_in_ref[...], jnp.concatenate([part[:64] for part in sorted_rows]))
    load.wait()
    upstream = dot_last(w_out_ref[...], jnp.concatenate([part[64:] for part in sorted_rows]))
    square = v * v
    half = 0.5 * jnp.tanh(v * (GELU_A + (GELU_A * GELU_B) * square)) + 0.5
    value = v * half
    slope = half + (value - value * half) * ((2.0 * GELU_A) + (6.0 * GELU_A * GELU_B) * square)
    hid = value.astype(BF)
    grad = (slope * upstream).astype(BF)
    hid_ref[...] = hid
    grad_ref[...] = grad
    buffer[:, 0, :] = dot_first(hid, w_out_ref[...]).astype(BF)
    buffer[:, 1, :] = dot_first(grad, w_in_ref[...]).astype(BF)
    copy = pltpu.make_async_copy(buffer, out_ref, sems.at[1])
    copy.start()
    copy.wait()


def logit_kernel(
    tokens_ref, grad_hbm, dispatch_ref, combine_ref, own_ref, parts_ref,
    slot_ref, logit_ref, term_ref, grad, sem,
):
    copy = pltpu.make_async_copy(grad_hbm, grad, sem)
    copy.start()
    tokens = tokens_ref[...]
    row = lax.broadcasted_iota(jnp.int32, (128, 512), 0)
    col = lax.broadcasted_iota(jnp.int32, (128, 512), 1) & 127
    adder = (col == 2 * (row & 63) + (row >> 6)).astype(BF)
    slots = jnp.dot(
        adder, parts_ref.reshape(512, 1280)[...], preferred_element_type=F32
    ).astype(BF)
    slot_out, slot_in_grad = slots[:64], slots[64:]
    slot_ref[...] = slot_in_grad
    row = lax.broadcasted_iota(jnp.int32, (64, 64), 0)
    col = lax.broadcasted_iota(jnp.int32, (64, 64), 1)
    stat = jnp.sum(
        jnp.where(row == col, dot_last(own_ref[...], slot_in_grad), 0.0), axis=0, keepdims=True
    )
    slot_part = dispatch_ref[...] * (dot_last(tokens, slot_in_grad) - stat)
    copy.wait()
    combine = combine_ref[...]
    combine_grad = dot_last(grad[...], slot_out)
    mean = jnp.sum(combine * combine_grad, axis=1, keepdims=True)
    logit_grad = (slot_part + combine * (combine_grad - mean)).astype(BF)
    logit_ref[...] = logit_grad
    term_ref.reshape(64, 1280)[...] = dot_first(logit_grad, tokens).astype(BF)


image_slots = on_core(
    image_kernel,
    (
        shape(192, 64, dtype=F32),
        shape(192, 64, dtype=F32),
        shape(64, 1280),
        shape(4, 64, 2, 1280),
    ),
    (HBM,) * 4,
    (
        pltpu.VMEM((192, 1280), BF),
        pltpu.VMEM((192, 64), F32),
        pltpu.VMEM((192, 64), F32),
        pltpu.VMEM((64, 1280), BF),
        pltpu.VMEM((64, 2, 1280), BF),
        pltpu.SemaphoreType.DMA((8,)),
    ),
    {2: HBM},
    grant=63_000_000,
)
experts = on_core(
    expert_kernel,
    (shape(640, 256), shape(640, 256), shape(256, 2, 1280)),
    (VMEM, VMEM, HBM),
    (
        pltpu.VMEM((256, 2, 1280), BF),
        pltpu.VMEM((640, 1280), BF),
        pltpu.SemaphoreType.DMA((2,)),
    ),
    {2: HBM, 3: HBM},
    {3: 2},
    grant=48 * 2**20,
)
logits_back = on_core(
    logit_kernel,
    (shape(64, 1280), shape(192, 64), shape(32, 2, 1280)),
    (VMEM,) * 3,
    (pltpu.VMEM((192, 1280), BF), pltpu.SemaphoreType.DMA(())),
    {1: HBM},
)


def exchange(blocks, axes):
    return lax.all_to_all(blocks, axes, split_axis=0, concat_axis=0, tiled=True)


def swap(value):
    return lax.ppermute(value, "core", SWAP)


def dot(spec, left, right):
    return jnp.einsum(spec, left, right, preferred_element_type=F32)


def local(tokens, grad_out, router, w_in, w_out):
    tokens, grad_out, w_in, w_out = tokens[0], grad_out[0], w_in[0], w_out[0]
    all_in = jnp.concatenate([w_in, swap(w_in)])
    all_out = jnp.concatenate([w_out, swap(w_out)])
    dispatch, combine, own_in, spent = image_slots(tokens, router.T, grad_out)
    spent = spent.reshape(256, 2, 1280)
    blocks = exchange(spent, CHIPS)
    hid, preact_grad, partial = experts(blocks, all_in, all_out, spent)
    parts = exchange(partial, CHIPS)
    d_in = dot("hi,id->hd", preact_grad, blocks[:, 0])
    d_out = dot("hi,id->hd", hid, blocks[:, 1])
    d_w_in = (d_in[:320] + swap(d_in[320:].astype(BF)).astype(F32)).astype(BF)
    d_w_out = (d_out[:320] + swap(d_out[320:].astype(BF)).astype(F32)).astype(BF)
    parts, d_w_in, d_w_out = lax.optimization_barrier((parts, d_w_in, d_w_out))
    slot_in_grad, logit_grad, term = logits_back(
        tokens, grad_out, dispatch, combine, own_in, parts
    )
    d_tokens = (
        dot("ms,ds->md", logit_grad, router)
        + dot("ms,sd->md", dispatch.astype(BF), slot_in_grad)
    ).astype(BF)
    term, d_tokens = lax.optimization_barrier((exchange(term, PLANE), d_tokens))
    term = jnp.sum(term.astype(F32), axis=0).astype(BF)
    term = exchange(jnp.broadcast_to(term[None], (16, 2, 1280)), LINE)
    term = jnp.sum(term.astype(F32), axis=0).astype(BF)
    term = exchange(jnp.broadcast_to(term[None], (32, 2, 1280)), PLANE)
    d_router = term.reshape(64, 1280).T
    return (d_tokens[None], d_router, d_w_in[None], d_w_out[None])


def solution(mesh):
    fine = Mesh(
        mesh.devices.reshape(4, 2, 2, 4, 8), ("y_lo", "core", "y_hi", "x", "z")
    )
    image = P(DP + EXPERT, None, None)
    unit = P(EXPERT, DP, None)
    return jax.shard_map(
        local,
        mesh=fine,
        in_specs=(image, image, P(), unit, unit),
        out_specs=(image, P(), unit, unit),
        check_vma=False,
    )
```

```python
import math

import jax
import jax.numpy as jnp
from jax import lax
from jax.experimental import pallas as pl
from jax.experimental.pallas import tpu as pltpu
from jax.sharding import Mesh, PartitionSpec as P

SWAP = [(0, 1), (1, 0)]
DP = ("y_pair", "y_side", "core")
EXPERT = ("y_hi", "x", "z")
CHIPS = ("y_pair",) + EXPERT
PLANE = ("x", "z")
LINE = ("y_pair", "y_side", "core", "y_hi")
BF = jnp.bfloat16
F32 = jnp.float32


VMEM = pl.BlockSpec(memory_space=pltpu.VMEM)
HBM = pl.BlockSpec(memory_space=pltpu.HBM)
GELU_A = math.sqrt(2.0 / math.pi)
GELU_B = 0.044715


def dot_last(left, right):
    return lax.dot_general(
        left, right, (((1,), (1,)), ((), ())), preferred_element_type=F32
    )


def dot_first(left, right):
    return lax.dot_general(
        left, right, (((0,), (0,)), ((), ())), preferred_element_type=F32
    )


def on_core(kernel, outs, out_specs, scratch=(), in_specs=None, aliases=None, grant=32 * 2**20):
    def call(*args):
        return pl.pallas_call(
            kernel,
            out_shape=outs,
            in_specs=[(in_specs or {}).get(i, VMEM) for i in range(len(args))],
            out_specs=out_specs,
            scratch_shapes=list(scratch),
            input_output_aliases=aliases or {},
            compiler_params=pltpu.CompilerParams(vmem_limit_bytes=grant),
        )(*args)

    return call


def shape(*dims, dtype=BF):
    return jax.ShapeDtypeStruct(dims, dtype)


def image_kernel(
    tokens_ref, router_ref, grad_hbm, dispatch_hbm, combine_hbm, own_hbm, out_ref,
    grad, dispatch_ref, combine_ref, own_ref, pair, sems,
):
    copy = pltpu.make_async_copy(grad_hbm, grad, sems.at[4])
    copy.start()
    tokens = tokens_ref[...]
    logits = dot_last(tokens, router_ref[...])
    dispatch = jnp.exp(logits - jnp.max(logits, axis=0, keepdims=True))
    dispatch = dispatch / jnp.sum(dispatch, axis=0, keepdims=True)
    dispatch_ref[...] = dispatch
    own_in = dot_first(dispatch.astype(BF), tokens).astype(BF)
    own_ref[...] = own_in
    copies = [
        pltpu.make_async_copy(dispatch_ref, dispatch_hbm, sems.at[5]),
        pltpu.make_async_copy(own_ref, own_hbm, sems.at[6]),
    ]
    for early in copies:
        early.start()
    pair[:, 0, :] = own_in
    combine = jnp.exp(logits - jnp.max(logits, axis=1, keepdims=True))
    combine = combine / jnp.sum(combine, axis=1, keepdims=True)
    combine_ref[...] = combine
    copies.append(pltpu.make_async_copy(combine_ref, combine_hbm, sems.at[7]))
    copies[-1].start()
    copy.wait()
    pair[:, 1, :] = dot_first(combine.astype(BF), grad[...]).astype(BF)
    late = [pltpu.make_async_copy(pair, out_ref.at[i], sems.at[i]) for i in range(2)]
    for each in late:
        each.start()
    for each in copies + late:
        each.wait()


def expert_kernel(*refs):
    *blocks, w_in_ref, w_out_ref, hid_ref, grad_ref = refs[: len(refs) // 2 + 2]
    outs = refs[len(refs) // 2 + 2 :]
    row = lax.broadcasted_iota(jnp.int32, (128, 128), 0)
    col = lax.broadcasted_iota(jnp.int32, (128, 128), 1)
    sort = (col == 2 * (row & 63) + (row >> 6)).astype(BF)
    sorted_rows = [
        jnp.dot(
            sort, ref.reshape(2 * ref.shape[0], 1280)[pl.ds(at, 128)], preferred_element_type=F32
        ).astype(BF)
        for ref in blocks
        for at in range(0, 2 * ref.shape[0], 128)
    ]
    v = dot_last(w_in_ref[...], jnp.concatenate([part[:64] for part in sorted_rows]))
    upstream = dot_last(w_out_ref[...], jnp.concatenate([part[64:] for part in sorted_rows]))
    square = v * v
    half = 0.5 * jnp.tanh(v * (GELU_A + (GELU_A * GELU_B) * square)) + 0.5
    value = v * half
    slope = half + (value - value * half) * ((2.0 * GELU_A) + (6.0 * GELU_A * GELU_B) * square)
    hid = value.astype(BF)
    grad = (slope * upstream).astype(BF)
    hid_ref[...] = hid
    grad_ref[...] = grad
    for kind, rows in enumerate((dot_first(hid, w_out_ref[...]), dot_first(grad, w_in_ref[...]))):
        rows = rows.astype(BF)
        at = 0
        for ref in outs:
            ref[:, kind, :] = rows[at : at + ref.shape[0]]
            at += ref.shape[0]


def logit_kernel(
    tokens_ref, grad_hbm, dispatch_ref, combine_ref, own_ref, parts_ref,
    slot_ref, logit_ref, term_ref, grad, sem,
):
    copy = pltpu.make_async_copy(grad_hbm, grad, sem)
    copy.start()
    tokens = tokens_ref[...]
    row = lax.broadcasted_iota(jnp.int32, (128, 256), 0)
    col = lax.broadcasted_iota(jnp.int32, (128, 256), 1) & 127
    adder = (col == 2 * (row & 63) + (row >> 6)).astype(BF)
    slots = jnp.dot(
        adder, parts_ref.reshape(256, 1280)[...], preferred_element_type=F32
    ).astype(BF)
    slot_out, slot_in_grad = slots[:64], slots[64:]
    slot_ref[...] = slot_in_grad
    row = lax.broadcasted_iota(jnp.int32, (64, 64), 0)
    col = lax.broadcasted_iota(jnp.int32, (64, 64), 1)
    stat = jnp.sum(
        jnp.where(row == col, dot_last(own_ref[...], slot_in_grad), 0.0), axis=0, keepdims=True
    )
    slot_part = dispatch_ref[...] * (dot_last(tokens, slot_in_grad) - stat)
    copy.wait()
    combine = combine_ref[...]
    combine_grad = dot_last(grad[...], slot_out)
    mean = jnp.sum(combine * combine_grad, axis=1, keepdims=True)
    logit_grad = (slot_part + combine * (combine_grad - mean)).astype(BF)
    logit_ref[...] = logit_grad
    term_ref.reshape(64, 1280)[...] = dot_first(logit_grad, tokens).astype(BF)


image_slots = on_core(
    image_kernel,
    (
        shape(192, 64, dtype=F32),
        shape(192, 64, dtype=F32),
        shape(64, 1280),
        shape(2, 64, 2, 1280),
    ),
    (HBM,) * 4,
    (
        pltpu.VMEM((192, 1280), BF),
        pltpu.VMEM((192, 64), F32),
        pltpu.VMEM((192, 64), F32),
        pltpu.VMEM((64, 1280), BF),
        pltpu.VMEM((64, 2, 1280), BF),
        pltpu.SemaphoreType.DMA((8,)),
    ),
    {2: HBM},
    grant=63_000_000,
)
ACTS = (shape(640, 128), shape(640, 128))
experts_near = on_core(expert_kernel, ACTS + (shape(128, 2, 1280),), (VMEM,) * 3)
experts_far = on_core(expert_kernel, ACTS + (shape(64, 2, 1280),) * 2, (VMEM,) * 4)
logits_back = on_core(
    logit_kernel,
    (shape(64, 1280), shape(192, 64), shape(32, 2, 1280)),
    (VMEM,) * 3,
    (pltpu.VMEM((192, 1280), BF), pltpu.SemaphoreType.DMA(())),
    {1: HBM},
)


def exchange(blocks, axes):
    return lax.all_to_all(blocks, axes, split_axis=0, concat_axis=0, tiled=True)


def across(value):
    return lax.ppermute(value, "y_side", SWAP)


def swap(value):
    return lax.ppermute(value, "core", SWAP)


def dot(spec, left, right):
    return jnp.einsum(spec, left, right, preferred_element_type=F32)


def local(tokens, grad_out, router, w_in, w_out):
    tokens, grad_out, w_in, w_out = tokens[0], grad_out[0], w_in[0], w_out[0]
    all_in = jnp.concatenate([w_in, swap(w_in)])
    all_out = jnp.concatenate([w_out, swap(w_out)])
    dispatch, combine, own_in, spent = image_slots(tokens, router.T, grad_out)
    near = exchange(spent.reshape(128, 2, 1280), CHIPS)
    far = (across(near[:64]), across(near[64:]))
    hid_near, grad_near, part_near = experts_near(near, all_in, all_out)
    hid_far, grad_far, *part_far = experts_far(*far, all_in, all_out)
    part_got = jnp.concatenate([across(part) for part in part_far])
    partial = (part_near.astype(F32) + part_got.astype(F32)).astype(BF)
    parts = exchange(partial, CHIPS)
    blocks = jnp.concatenate((near,) + far)
    d_in = dot("hi,id->hd", jnp.concatenate([grad_near, grad_far], axis=1), blocks[:, 0])
    d_out = dot("hi,id->hd", jnp.concatenate([hid_near, hid_far], axis=1), blocks[:, 1])
    d_w_in = (d_in[:320] + swap(d_in[320:].astype(BF)).astype(F32)).astype(BF)
    d_w_out = (d_out[:320] + swap(d_out[320:].astype(BF)).astype(F32)).astype(BF)
    parts, d_w_in, d_w_out = lax.optimization_barrier((parts, d_w_in, d_w_out))
    slot_in_grad, logit_grad, term = logits_back(
        tokens, grad_out, dispatch, combine, own_in, parts
    )
    d_tokens = (
        dot("ms,ds->md", logit_grad, router)
        + dot("ms,sd->md", dispatch.astype(BF), slot_in_grad)
    ).astype(BF)
    term, d_tokens = lax.optimization_barrier((exchange(term, PLANE), d_tokens))
    term = jnp.sum(term.astype(F32), axis=0).astype(BF)
    term = exchange(jnp.broadcast_to(term[None], (16, 2, 1280)), LINE)
    term = jnp.sum(term.astype(F32), axis=0).astype(BF)
    term = exchange(jnp.broadcast_to(term[None], (32, 2, 1280)), PLANE)
    d_router = term.reshape(64, 1280).T
    return (d_tokens[None], d_router, d_w_in[None], d_w_out[None])


def solution(mesh):
    fine = Mesh(
        mesh.devices.reshape(2, 2, 2, 2, 4, 8), ("y_pair", "y_side", "core", "y_hi", "x", "z")
    )
    image = P(DP + EXPERT, None, None)
    unit = P(EXPERT, DP, None)
    return jax.shard_map(
        local,
        mesh=fine,
        in_specs=(image, image, P(), unit, unit),
        out_specs=(image, P(), unit, unit),
        check_vma=False,
    )
```

```python
import math

import jax
import jax.numpy as jnp
from jax import lax
from jax.experimental import pallas as pl
from jax.experimental.pallas import tpu as pltpu
from jax.sharding import Mesh, PartitionSpec as P

SWAP = [(0, 1), (1, 0)]
DP = ("y_lo", "core")
EXPERT = ("y_hi", "x", "z")
CHIPS = ("y_lo",) + EXPERT
PLANE = ("x", "z")
LINE = ("y_lo", "core", "y_hi")
BF = jnp.bfloat16
F32 = jnp.float32


VMEM = pl.BlockSpec(memory_space=pltpu.VMEM)
HBM = pl.BlockSpec(memory_space=pltpu.HBM)
GELU_A = math.sqrt(2.0 / math.pi)
GELU_B = 0.044715


def dot_last(left, right):
    return lax.dot_general(
        left, right, (((1,), (1,)), ((), ())), preferred_element_type=F32
    )


def dot_first(left, right):
    return lax.dot_general(
        left, right, (((0,), (0,)), ((), ())), preferred_element_type=F32
    )


def on_core(kernel, outs, out_specs, scratch=(), in_specs=None, aliases=None, grant=32 * 2**20):
    def call(*args):
        return pl.pallas_call(
            kernel,
            out_shape=outs,
            in_specs=[(in_specs or {}).get(i, VMEM) for i in range(len(args))],
            out_specs=out_specs,
            scratch_shapes=list(scratch),
            input_output_aliases=aliases or {},
            compiler_params=pltpu.CompilerParams(vmem_limit_bytes=grant),
        )(*args)

    return call


def shape(*dims, dtype=BF):
    return jax.ShapeDtypeStruct(dims, dtype)


def image_kernel(
    tokens_ref, router_ref, grad_hbm, dispatch_hbm, combine_hbm, own_hbm, out_ref,
    grad, dispatch_ref, combine_ref, own_ref, pair, sems,
):
    copy = pltpu.make_async_copy(grad_hbm, grad, sems.at[4])
    copy.start()
    tokens = tokens_ref[...]
    logits = dot_last(tokens, router_ref[...])
    dispatch = jnp.exp(logits - jnp.max(logits, axis=0, keepdims=True))
    dispatch = dispatch / jnp.sum(dispatch, axis=0, keepdims=True)
    dispatch_ref[...] = dispatch
    own_in = dot_first(dispatch.astype(BF), tokens).astype(BF)
    own_ref[...] = own_in
    copies = [
        pltpu.make_async_copy(dispatch_ref, dispatch_hbm, sems.at[5]),
        pltpu.make_async_copy(own_ref, own_hbm, sems.at[6]),
    ]
    for early in copies:
        early.start()
    pair[:, 0, :] = own_in
    combine = jnp.exp(logits - jnp.max(logits, axis=1, keepdims=True))
    combine = combine / jnp.sum(combine, axis=1, keepdims=True)
    combine_ref[...] = combine
    copies.append(pltpu.make_async_copy(combine_ref, combine_hbm, sems.at[7]))
    copies[-1].start()
    copy.wait()
    pair[:, 1, :] = dot_first(combine.astype(BF), grad[...]).astype(BF)
    late = [pltpu.make_async_copy(pair, out_ref.at[i], sems.at[i]) for i in range(4)]
    for each in late:
        each.start()
    for each in copies + late:
        each.wait()


def expert_kernel(
    blocks_ref, w_in_ref, w_out_hbm, spent_ref, hid_ref, grad_ref, out_ref, buffer, w_out_ref, sems
):
    del spent_ref
    load = pltpu.make_async_copy(w_out_hbm, w_out_ref, sems.at[0])
    load.start()
    row = lax.broadcasted_iota(jnp.int32, (128, 128), 0)
    col = lax.broadcasted_iota(jnp.int32, (128, 128), 1)
    sort = (col == 2 * (row & 63) + (row >> 6)).astype(BF)
    rows = blocks_ref.reshape(512, 1280)
    sorted_rows = [
        jnp.dot(sort, rows[pl.ds(at, 128)], preferred_element_type=F32).astype(BF)
        for at in range(0, 512, 128)
    ]
    v = dot_last(w_in_ref[...], jnp.concatenate([part[:64] for part in sorted_rows]))
    load.wait()
    upstream = dot_last(w_out_ref[...], jnp.concatenate([part[64:] for part in sorted_rows]))
    square = v * v
    half = 0.5 * jnp.tanh(v * (GELU_A + (GELU_A * GELU_B) * square)) + 0.5
    value = v * half
    slope = half + (value - value * half) * ((2.0 * GELU_A) + (6.0 * GELU_A * GELU_B) * square)
    hid = value.astype(BF)
    grad = (slope * upstream).astype(BF)
    hid_ref[...] = hid
    grad_ref[...] = grad
    copies = []
    for i in range(2):
        part = pl.ds(i * 128, 128)
        buffer[part, 0, :] = dot_first(hid[:, i * 128 : i * 128 + 128], w_out_ref[...]).astype(BF)
        buffer[part, 1, :] = dot_first(grad[:, i * 128 : i * 128 + 128], w_in_ref[...]).astype(BF)
        copies.append(pltpu.make_async_copy(buffer.at[part], out_ref.at[part], sems.at[1 + i]))
        copies[-1].start()
    for copy in copies:
        copy.wait()


def logit_kernel(
    tokens_ref, grad_hbm, dispatch_ref, combine_ref, own_ref, parts_ref,
    slot_ref, logit_ref, term_ref, grad, sem,
):
    copy = pltpu.make_async_copy(grad_hbm, grad, sem)
    copy.start()
    tokens = tokens_ref[...]
    row = lax.broadcasted_iota(jnp.int32, (128, 512), 0)
    col = lax.broadcasted_iota(jnp.int32, (128, 512), 1) & 127
    adder = (col == 2 * (row & 63) + (row >> 6)).astype(BF)
    slots = jnp.dot(
        adder, parts_ref.reshape(512, 1280)[...], preferred_element_type=F32
    ).astype(BF)
    slot_out, slot_in_grad = slots[:64], slots[64:]
    slot_ref[...] = slot_in_grad
    row = lax.broadcasted_iota(jnp.int32, (64, 64), 0)
    col = lax.broadcasted_iota(jnp.int32, (64, 64), 1)
    stat = jnp.sum(
        jnp.where(row == col, dot_last(own_ref[...], slot_in_grad), 0.0), axis=0, keepdims=True
    )
    slot_part = dispatch_ref[...] * (dot_last(tokens, slot_in_grad) - stat)
    copy.wait()
    combine = combine_ref[...]
    combine_grad = dot_last(grad[...], slot_out)
    mean = jnp.sum(combine * combine_grad, axis=1, keepdims=True)
    logit_grad = (slot_part + combine * (combine_grad - mean)).astype(BF)
    logit_ref[...] = logit_grad
    term_ref.reshape(64, 1280)[...] = dot_first(logit_grad, tokens).astype(BF)


image_slots = on_core(
    image_kernel,
    (
        shape(192, 64, dtype=F32),
        shape(192, 64, dtype=F32),
        shape(64, 1280),
        shape(4, 64, 2, 1280),
    ),
    (HBM,) * 4,
    (
        pltpu.VMEM((192, 1280), BF),
        pltpu.VMEM((192, 64), F32),
        pltpu.VMEM((192, 64), F32),
        pltpu.VMEM((64, 1280), BF),
        pltpu.VMEM((64, 2, 1280), BF),
        pltpu.SemaphoreType.DMA((8,)),
    ),
    {2: HBM},
    grant=63_000_000,
)
experts = on_core(
    expert_kernel,
    (shape(640, 256), shape(640, 256), shape(256, 2, 1280)),
    (VMEM, VMEM, HBM),
    (
        pltpu.VMEM((256, 2, 1280), BF),
        pltpu.VMEM((640, 1280), BF),
        pltpu.SemaphoreType.DMA((3,)),
    ),
    {2: HBM, 3: HBM},
    {3: 2},
    grant=48 * 2**20,
)
logits_back = on_core(
    logit_kernel,
    (shape(64, 1280), shape(192, 64), shape(32, 2, 1280)),
    (VMEM,) * 3,
    (pltpu.VMEM((192, 1280), BF), pltpu.SemaphoreType.DMA(())),
    {1: HBM},
)


def exchange(blocks, axes):
    return lax.all_to_all(blocks, axes, split_axis=0, concat_axis=0, tiled=True)


def swap(value):
    return lax.ppermute(value, "core", SWAP)


def dot(spec, left, right):
    return jnp.einsum(spec, left, right, preferred_element_type=F32)


def local(tokens, grad_out, router, w_in, w_out):
    tokens, grad_out, w_in, w_out = tokens[0], grad_out[0], w_in[0], w_out[0]
    all_in = jnp.concatenate([w_in, swap(w_in)])
    all_out = jnp.concatenate([w_out, swap(w_out)])
    dispatch, combine, own_in, spent = image_slots(tokens, router.T, grad_out)
    spent = spent.reshape(256, 2, 1280)
    blocks = exchange(spent, CHIPS)
    hid, preact_grad, partial = experts(blocks, all_in, all_out, spent)
    parts = exchange(partial, CHIPS)
    d_in = dot("hi,id->hd", preact_grad, blocks[:, 0])
    d_out = dot("hi,id->hd", hid, blocks[:, 1])
    d_w_in = (d_in[:320] + swap(d_in[320:].astype(BF)).astype(F32)).astype(BF)
    d_w_out = (d_out[:320] + swap(d_out[320:].astype(BF)).astype(F32)).astype(BF)
    parts, d_w_in, d_w_out = lax.optimization_barrier((parts, d_w_in, d_w_out))
    slot_in_grad, logit_grad, term = logits_back(
        tokens, grad_out, dispatch, combine, own_in, parts
    )
    d_tokens = (
        dot("ms,ds->md", logit_grad, router)
        + dot("ms,sd->md", dispatch.astype(BF), slot_in_grad)
    ).astype(BF)
    term, d_tokens = lax.optimization_barrier((exchange(term, PLANE), d_tokens))
    term = jnp.sum(term.astype(F32), axis=0).astype(BF)
    term = exchange(jnp.broadcast_to(term[None], (16, 2, 1280)), LINE)
    term = jnp.sum(term.astype(F32), axis=0).astype(BF)
    term = exchange(jnp.broadcast_to(term[None], (32, 2, 1280)), PLANE)
    d_router = term.reshape(64, 1280).T
    return (d_tokens[None], d_router, d_w_in[None], d_w_out[None])


def solution(mesh):
    fine = Mesh(
        mesh.devices.reshape(4, 2, 2, 4, 8), ("y_lo", "core", "y_hi", "x", "z")
    )
    image = P(DP + EXPERT, None, None)
    unit = P(EXPERT, DP, None)
    return jax.shard_map(
        local,
        mesh=fine,
        in_specs=(image, image, P(), unit, unit),
        out_specs=(image, P(), unit, unit),
        check_vma=False,
    )
```

```python
import math

import jax
import jax.numpy as jnp
from jax import lax
from jax.experimental import pallas as pl
from jax.experimental.pallas import tpu as pltpu
from jax.sharding import Mesh, PartitionSpec as P

SWAP = [(0, 1), (1, 0)]
DP = ("y_lo", "core")
EXPERT = ("y_hi", "x", "z")
CHIPS = ("y_lo",) + EXPERT
PLANE = ("x", "z")
LINE = ("y_lo", "core", "y_hi")
BF = jnp.bfloat16
F32 = jnp.float32


VMEM = pl.BlockSpec(memory_space=pltpu.VMEM)
HBM = pl.BlockSpec(memory_space=pltpu.HBM)
GELU_A = math.sqrt(2.0 / math.pi)
GELU_B = 0.044715


def dot_last(left, right):
    return lax.dot_general(
        left, right, (((1,), (1,)), ((), ())), preferred_element_type=F32
    )


def dot_first(left, right):
    return lax.dot_general(
        left, right, (((0,), (0,)), ((), ())), preferred_element_type=F32
    )


def on_core(kernel, outs, out_specs, scratch=(), in_specs=None, aliases=None, grant=32 * 2**20):
    def call(*args):
        return pl.pallas_call(
            kernel,
            out_shape=outs,
            in_specs=[(in_specs or {}).get(i, VMEM) for i in range(len(args))],
            out_specs=out_specs,
            scratch_shapes=list(scratch),
            input_output_aliases=aliases or {},
            compiler_params=pltpu.CompilerParams(vmem_limit_bytes=grant),
        )(*args)

    return call


def shape(*dims, dtype=BF):
    return jax.ShapeDtypeStruct(dims, dtype)


def image_kernel(
    tokens_ref, router_ref, grad_hbm, dispatch_hbm, combine_hbm, own_hbm, out_ref,
    grad, dispatch_ref, combine_ref, own_ref, pair, sems,
):
    copy = pltpu.make_async_copy(grad_hbm, grad, sems.at[4])
    copy.start()
    tokens = tokens_ref[...]
    logits = dot_last(tokens, router_ref[...])
    dispatch = jnp.exp(logits - jnp.max(logits, axis=0, keepdims=True))
    dispatch = dispatch / jnp.sum(dispatch, axis=0, keepdims=True)
    dispatch_ref[...] = dispatch
    own_in = dot_first(dispatch.astype(BF), tokens).astype(BF)
    own_ref[...] = own_in
    copies = [
        pltpu.make_async_copy(dispatch_ref, dispatch_hbm, sems.at[5]),
        pltpu.make_async_copy(own_ref, own_hbm, sems.at[6]),
    ]
    for early in copies:
        early.start()
    pair[:, 0, :] = own_in
    combine = jnp.exp(logits - jnp.max(logits, axis=1, keepdims=True))
    combine = combine / jnp.sum(combine, axis=1, keepdims=True)
    combine_ref[...] = combine
    copies.append(pltpu.make_async_copy(combine_ref, combine_hbm, sems.at[7]))
    copies[-1].start()
    copy.wait()
    pair[:, 1, :] = dot_first(combine.astype(BF), grad[...]).astype(BF)
    late = [pltpu.make_async_copy(pair, out_ref.at[i], sems.at[i]) for i in range(4)]
    for each in late:
        each.start()
    for each in copies + late:
        each.wait()


def expert_kernel(
    blocks_ref, w_in_ref, w_out_hbm, spent_ref, hid_ref, grad_ref, out_ref, buffer, w_out_ref, sems
):
    del spent_ref
    load = pltpu.make_async_copy(w_out_hbm, w_out_ref, sems.at[0])
    load.start()
    row = lax.broadcasted_iota(jnp.int32, (128, 128), 0)
    col = lax.broadcasted_iota(jnp.int32, (128, 128), 1)
    sort = (col == 2 * (row & 63) + (row >> 6)).astype(BF)
    rows = blocks_ref.reshape(512, 1280)
    sorted_rows = [
        jnp.dot(sort, rows[pl.ds(at, 128)], preferred_element_type=F32).astype(BF)
        for at in range(0, 512, 128)
    ]
    v = dot_last(w_in_ref[...], jnp.concatenate([part[:64] for part in sorted_rows]))
    load.wait()
    upstream = dot_last(w_out_ref[...], jnp.concatenate([part[64:] for part in sorted_rows]))
    square = v * v
    half = 0.5 * jnp.tanh(v * (GELU_A + (GELU_A * GELU_B) * square)) + 0.5
    value = v * half
    slope = half + (value - value * half) * ((2.0 * GELU_A) + (6.0 * GELU_A * GELU_B) * square)
    hid = value.astype(BF)
    grad = (slope * upstream).astype(BF)
    hid_ref[...] = hid
    grad_ref[...] = grad
    copies = []
    for i in range(2):
        part = pl.ds(i * 128, 128)
        buffer[part, 0, :] = dot_first(hid[:, i * 128 : i * 128 + 128], w_out_ref[...]).astype(BF)
        buffer[part, 1, :] = dot_first(grad[:, i * 128 : i * 128 + 128], w_in_ref[...]).astype(BF)
        copies.append(pltpu.make_async_copy(buffer.at[part], out_ref.at[part], sems.at[1 + i]))
        copies[-1].start()
    for copy in copies:
        copy.wait()


def logit_kernel(
    tokens_ref, grad_hbm, dispatch_ref, combine_ref, own_ref, parts_ref,
    slot_ref, logit_ref, term_ref, grad, sem,
):
    copy = pltpu.make_async_copy(grad_hbm, grad, sem)
    copy.start()
    tokens = tokens_ref[...]
    row = lax.broadcasted_iota(jnp.int32, (128, 512), 0)
    col = lax.broadcasted_iota(jnp.int32, (128, 512), 1) & 127
    adder = (col == 2 * (row & 63) + (row >> 6)).astype(BF)
    slots = jnp.dot(
        adder, parts_ref.reshape(512, 1280)[...], preferred_element_type=F32
    ).astype(BF)
    slot_out, slot_in_grad = slots[:64], slots[64:]
    slot_ref[...] = slot_in_grad
    row = lax.broadcasted_iota(jnp.int32, (64, 64), 0)
    col = lax.broadcasted_iota(jnp.int32, (64, 64), 1)
    stat = jnp.sum(
        jnp.where(row == col, dot_last(own_ref[...], slot_in_grad), 0.0), axis=0, keepdims=True
    )
    slot_part = dispatch_ref[...] * (dot_last(tokens, slot_in_grad) - stat)
    copy.wait()
    combine = combine_ref[...]
    combine_grad = dot_last(grad[...], slot_out)
    mean = jnp.sum(combine * combine_grad, axis=1, keepdims=True)
    logit_grad = (slot_part + combine * (combine_grad - mean)).astype(BF)
    logit_ref[...] = logit_grad
    term_ref.reshape(64, 1280)[...] = dot_first(logit_grad, tokens).astype(BF)


image_slots = on_core(
    image_kernel,
    (
        shape(192, 64, dtype=F32),
        shape(192, 64, dtype=F32),
        shape(64, 1280),
        shape(4, 64, 2, 1280),
    ),
    (HBM,) * 4,
    (
        pltpu.VMEM((192, 1280), BF),
        pltpu.VMEM((192, 64), F32),
        pltpu.VMEM((192, 64), F32),
        pltpu.VMEM((64, 1280), BF),
        pltpu.VMEM((64, 2, 1280), BF),
        pltpu.SemaphoreType.DMA((8,)),
    ),
    {2: HBM},
    grant=63_000_000,
)
experts = on_core(
    expert_kernel,
    (shape(640, 256), shape(640, 256), shape(256, 2, 1280)),
    (VMEM, VMEM, HBM),
    (
        pltpu.VMEM((256, 2, 1280), BF),
        pltpu.VMEM((640, 1280), BF),
        pltpu.SemaphoreType.DMA((3,)),
    ),
    {2: HBM, 3: HBM},
    {3: 2},
    grant=48 * 2**20,
)
logits_back = on_core(
    logit_kernel,
    (shape(64, 1280), shape(192, 64), shape(32, 2, 1280)),
    (VMEM,) * 3,
    (pltpu.VMEM((192, 1280), BF), pltpu.SemaphoreType.DMA(())),
    {1: HBM},
)


def rows_kernel(blocks_ref, out_ref):
    out_ref[...] = blocks_ref.reshape(64, 1280)[...]


plain_rows = on_core(rows_kernel, shape(64, 1280), VMEM)


def exchange(blocks, axes):
    return lax.all_to_all(blocks, axes, split_axis=0, concat_axis=0, tiled=True)


def swap(value):
    return lax.ppermute(value, "core", SWAP)


def dot(spec, left, right):
    return jnp.einsum(spec, left, right, preferred_element_type=F32)


def local(tokens, grad_out, router, w_in, w_out):
    tokens, grad_out, w_in, w_out = tokens[0], grad_out[0], w_in[0], w_out[0]
    all_in = jnp.concatenate([w_in, swap(w_in)])
    all_out = jnp.concatenate([w_out, swap(w_out)])
    dispatch, combine, own_in, spent = image_slots(tokens, router.T, grad_out)
    spent = spent.reshape(256, 2, 1280)
    blocks = exchange(spent, CHIPS)
    hid, preact_grad, partial = experts(blocks, all_in, all_out, spent)
    parts = exchange(partial, CHIPS)
    d_in = dot("hi,id->hd", preact_grad, blocks[:, 0])
    d_out = dot("hi,id->hd", hid, blocks[:, 1])
    d_w_in = (d_in[:320] + swap(d_in[320:].astype(BF)).astype(F32)).astype(BF)
    d_w_out = (d_out[:320] + swap(d_out[320:].astype(BF)).astype(F32)).astype(BF)
    parts, d_w_in, d_w_out = lax.optimization_barrier((parts, d_w_in, d_w_out))
    slot_in_grad, logit_grad, term = logits_back(
        tokens, grad_out, dispatch, combine, own_in, parts
    )
    d_tokens = (
        dot("ms,ds->md", logit_grad, router)
        + dot("ms,sd->md", dispatch.astype(BF), slot_in_grad)
    ).astype(BF)
    term, d_tokens = lax.optimization_barrier((exchange(term, PLANE), d_tokens))
    term = jnp.sum(term.astype(F32), axis=0).astype(BF)
    term = exchange(jnp.broadcast_to(term[None], (16, 2, 1280)), LINE)
    term = jnp.sum(term.astype(F32), axis=0).astype(BF)
    term = exchange(jnp.broadcast_to(term[None], (32, 2, 1280)), PLANE)
    d_router = plain_rows(term).T
    return (d_tokens[None], d_router, d_w_in[None], d_w_out[None])


def solution(mesh):
    fine = Mesh(
        mesh.devices.reshape(4, 2, 2, 4, 8), ("y_lo", "core", "y_hi", "x", "z")
    )
    image = P(DP + EXPERT, None, None)
    unit = P(EXPERT, DP, None)
    return jax.shard_map(
        local,
        mesh=fine,
        in_specs=(image, image, P(), unit, unit),
        out_specs=(image, P(), unit, unit),
        check_vma=False,
    )
```
